32 devices in a mesh: slab: 2 (over x), row: 16 (over z, y, core).
Axes of the slice: x: 2, y: 2, z: 4, core: 2. Of those that a mesh axis runs over, the one named last changes fastest.
Arguments:
- slab: bfloat16 [32, 128, 128, 128], P(('slab', 'row')), parts along dimension 0, may hold values from -12 to 12
- row_factor: bfloat16 [32, 8], P('slab'), parts along dimension 0, may hold values from -1.5 to 1.5
- col_factor: bfloat16 [256, 8], P('slab'), parts along dimension 0, may hold values from -0.5 to 0.5
- det_row_factor: bfloat16 [256, 64], P('slab'), parts along dimension 0, may hold values from -0.5 to 0.5
- det_col_factor: bfloat16 [256, 64], P('slab'), parts along dimension 0, may hold values from -0.5 to 0.5
Outputs:
- scan_row_gram: float32 [32, 16], P('slab'), parts along dimension 0
- scan_col_gram: float32 [256, 128], P('slab'), parts along dimension 0
- det_row_gram: float32 [256, 128], P('slab'), parts along dimension 0
- det_col_gram: float32 [256, 128], P('slab'), parts along dimension 0
The draws below stay inside these ranges and needn't reach their ends.
There are 2 independent parts, one for each index of `slab`. The reference program is written for one: setup_inputs(seed, part) draws one part's arguments, and reference() takes and returns one part's arrays. A program takes and returns all parts, laid end to end along the dimension named above; each array names one. Nothing has to cross between parts.
All inputs are finite; a program needn't handle non-finite values.
Results may differ from the reference program's by a relative error of at most 0.0016.
Values may be sent and summed in bfloat16 or wider, within the bound.
No kernel may reach another device: no remote copies, remote signals or barrier semaphores. Data moves between devices by JAX's collectives and lax.ppermute only.
A program may use at most 64 MiB of HBM per device.

```python
import jax
import jax.numpy as jnp
from jax import lax

DETECTOR = 128
DET_RANK = 64
SCAN_RANK = 8
SCAN_COLS = 128
SCAN_ROWS = 16


def draw_slab(key, part):
    key = jax.random.fold_in(key, 11)
    pattern_key, weight_key, noise_key = jax.random.split(key, 3)
    shape = (SCAN_ROWS, SCAN_COLS, DETECTOR, DETECTOR)
    pattern = jax.random.normal(pattern_key, (1, 1, DETECTOR, DETECTOR), jnp.float32)
    weights = 1.0 + 0.5 * jax.random.normal(weight_key, (SCAN_ROWS, SCAN_COLS, 1, 1), jnp.float32)
    noise = jax.random.normal(noise_key, shape, jnp.float32)
    values = jnp.clip(weights * pattern + noise, -12.0, 12.0)
    return values.astype(jnp.bfloat16)


def bell_draw(rng, dims, scale, bound, dtype=jnp.bfloat16):
    return jnp.clip(scale * jax.random.normal(rng, dims, jnp.float32), -bound, bound).astype(dtype)


def setup_inputs(seed: int = 0, part: int = 0) -> dict:
    seeds = jax.random.split(jax.random.key(seed), 6)
    part_keys = jax.random.split(jax.random.fold_in(seeds[5], part), 6)
    return {
        "slab": draw_slab(jax.random.fold_in(jax.random.fold_in(seeds[5], part), 71), part),
        "row_factor": bell_draw(part_keys[1], (SCAN_ROWS, SCAN_RANK), SCAN_ROWS ** -0.5, 1.5),
        "col_factor": bell_draw(part_keys[2], (SCAN_COLS, SCAN_RANK), SCAN_COLS ** -0.5, 0.5),
        "det_row_factor": bell_draw(part_keys[3], (DETECTOR, DET_RANK), DETECTOR ** -0.5, 0.5),
        "det_col_factor": bell_draw(part_keys[4], (DETECTOR, DET_RANK), DETECTOR ** -0.5, 0.5),
    }


def reference(slab, row_factor, col_factor, det_row_factor, det_col_factor):
    col_weights = col_factor.astype(jnp.float32)
    det_rows = det_row_factor.astype(jnp.float32)

    def one_row(carry, inputs):
        image, weight_row = inputs
        col_sum, right_sum, left_sum = carry
        half_right = jnp.dot(image.reshape(SCAN_COLS * DETECTOR, DETECTOR), det_col_factor,
                             preferred_element_type=jnp.float32).astype(jnp.bfloat16)
        half_right = half_right.reshape(SCAN_COLS, DETECTOR, DET_RANK)
        half_left = jnp.einsum("ckl,ka->cla", image.astype(jnp.float32), det_rows).astype(jnp.bfloat16)
        cubes = jnp.einsum("ckb,ka->cab", half_right.astype(jnp.float32), det_rows).astype(jnp.bfloat16)
        row_unfold = jnp.einsum("cab,cj->jab", cubes.astype(jnp.float32), col_weights).astype(jnp.bfloat16)
        weights = weight_row.astype(jnp.float32)[:, None, None, None]
        col_sum = col_sum + weights * cubes.astype(jnp.float32)[None]
        right_cols = jnp.einsum("ckb,cj->jkb", half_right.astype(jnp.float32), col_weights)
        left_cols = jnp.einsum("cla,cj->jal", half_left.astype(jnp.float32), col_weights)
        right_sum = right_sum + weights * right_cols[None]
        left_sum = left_sum + weights * left_cols[None]
        return (col_sum, right_sum, left_sum), row_unfold

    initial = (jnp.zeros((SCAN_RANK, SCAN_COLS, DET_RANK, DET_RANK), jnp.float32),
               jnp.zeros((SCAN_RANK, SCAN_RANK, DETECTOR, DET_RANK), jnp.float32),
               jnp.zeros((SCAN_RANK, SCAN_RANK, DET_RANK, DETECTOR), jnp.float32))
    (col_sum, right_sum, left_sum), row_unfold = lax.scan(one_row, initial, (slab, row_factor))
    col_unfold = col_sum.astype(jnp.bfloat16).astype(jnp.float32)
    det_right = right_sum.astype(jnp.bfloat16).astype(jnp.float32)
    det_left = left_sum.astype(jnp.bfloat16).astype(jnp.float32)
    rows_flat = row_unfold.astype(jnp.float32)
    scan_scale = 1.0 / (SCAN_RANK * DET_RANK * DET_RANK)
    det_scale = 1.0 / (SCAN_RANK * SCAN_RANK * DET_RANK)
    scan_row_gram = jnp.einsum("rjab,sjab->rs", rows_flat, rows_flat) * scan_scale
    scan_col_gram = jnp.einsum("icab,idab->cd", col_unfold, col_unfold) * scan_scale
    det_row_gram = jnp.einsum("ijkb,ijmb->km", det_right, det_right) * det_scale
    det_col_gram = jnp.einsum("ijal,ijam->lm", det_left, det_left) * det_scale
    return (scan_row_gram, scan_col_gram, det_row_gram, det_col_gram)
```

```python
import functools

import jax
import jax.numpy as jnp
from jax import lax
from jax.experimental import pallas as pl
from jax.experimental.pallas import tpu as pltpu
from jax.sharding import PartitionSpec as P

DET_RANK = 64
SCAN_RANK = 8
SCAN_SCALE = 1.0 / (SCAN_RANK * DET_RANK * DET_RANK)
DET_SCALE = 1.0 / (SCAN_RANK * SCAN_RANK * DET_RANK)
LANES = 128
BF16 = jnp.bfloat16
F32 = jnp.float32
LAST = (((1,), (1,)), ((), ()))
FIRST = (((0,), (0,)), ((), ()))


def dot(x, y, dims=None):
    if dims is None:
        return jnp.dot(x, y, preferred_element_type=F32)
    return lax.dot_general(x, y, dims, preferred_element_type=F32)


def project(n, cuts, slab, cft_in, dt_in, vt_in, out, cft, dt, vt, images, right, left, arrived, ready):
    cols, pixels = slab.shape[0], slab.shape[1]
    pitch = cols + 1
    rank = dt.shape[0]
    own = rank // n
    cuts = [0, *cuts, cols]
    copies = [
        pltpu.make_async_copy(slab.at[pl.ds(a, b - a)], images.at[pl.ds(a, b - a)], arrived.at[i])
        for i, (a, b) in enumerate(zip(cuts, cuts[1:]))
    ]
    factors = [
        pltpu.make_async_copy(x, y, ready.at[i]) for i, (x, y) in enumerate([(dt_in, dt), (vt_in, vt), (cft_in, cft)])
    ]
    for copy in factors + copies:
        copy.start()
    for copy in factors:
        copy.wait()
    none = jnp.zeros((rank, pixels), BF16)
    dt2 = jnp.concatenate([jnp.concatenate([dt[...], none], 1), jnp.concatenate([none, dt[...]], 1)], 0)
    vt2 = jnp.concatenate([jnp.concatenate([vt[...], none], 1), jnp.concatenate([none, vt[...]], 1)], 0)
    tall = dt[...].T
    none = jnp.zeros_like(tall)
    dd = jnp.concatenate([jnp.concatenate([tall, none], 1), jnp.concatenate([none, tall], 1)], 0)
    for at, copy in enumerate(copies):
        copy.wait()
        for c in range(cuts[at], cuts[at + 1], 4):
            four = jnp.concatenate(
                [
                    jnp.concatenate([images[c], images[c + 1]], axis=1),
                    jnp.concatenate([images[c + 2], images[c + 3]], axis=1),
                ],
                axis=0,
            )
            rights = dot(vt2, four, LAST)
            lefts = dot(dt2, four)
            for i in range(2):
                for j in range(2):
                    at_c = pl.ds(c + 2 * i + j, rank, stride=pitch)
                    right[at_c, :] = rights[j * rank : (j + 1) * rank, i * pixels : (i + 1) * pixels]
                    left[at_c, :] = lefts[i * rank : (i + 1) * rank, j * pixels : (j + 1) * pixels]
    n_cube = own // 2 * cols
    n_part = own * SCAN_RANK
    pair = 2 * SCAN_RANK
    for p in range(n):
        for h in range(own // 2):
            b = p * own + 2 * h
            two_right = [right[pl.ds((b + k) * pitch, cols), :].astype(BF16) for k in range(2)]
            two_left = [left[pl.ds((b + k) * pitch, cols), :].astype(BF16) for k in range(2)]
            x = jnp.concatenate(two_right, axis=1)
            y = jnp.concatenate(two_left, axis=1)
            out[p, pl.ds(h * cols, cols), :] = dot(x, dd).astype(BF16)
            sums = dot(cft[...], x)
            out[p, pl.ds(n_cube + h * pair, pair), :] = jnp.concatenate(
                [sums[:, :pixels], sums[:, pixels:]], axis=0
            ).astype(BF16)
            sums = dot(cft[...], y)
            out[p, pl.ds(n_cube + n_part + h * pair, pair), :] = jnp.concatenate(
                [sums[:, :pixels], sums[:, pixels:]], axis=0
            ).astype(BF16)


def projections(n, cuts, slab, cft, dt, vt):
    cols, pixels = slab.shape[0], slab.shape[1]
    rank = dt.shape[0]
    own = rank // n
    rows = own // 2 * cols + 2 * own * SCAN_RANK
    in_vmem = pl.BlockSpec(memory_space=pltpu.VMEM)
    return pl.pallas_call(
        functools.partial(project, n, cuts),
        out_shape=jax.ShapeDtypeStruct((n, rows, pixels), BF16),
        in_specs=[pl.BlockSpec(memory_space=pl.ANY)] * 4,
        out_specs=in_vmem,
        scratch_shapes=[
            pltpu.VMEM(cft.shape, BF16),
            pltpu.VMEM(dt.shape, BF16),
            pltpu.VMEM(vt.shape, BF16),
            pltpu.VMEM(slab.shape, BF16),
            pltpu.VMEM((rank * (cols + 1), pixels), F32),
            pltpu.VMEM((rank * (cols + 1), pixels), F32),
            pltpu.SemaphoreType.DMA((len(cuts) + 1,)),
            pltpu.SemaphoreType.DMA((3,)),
        ],
        compiler_params=pltpu.CompilerParams(vmem_limit_bytes=56 << 20),
    )(slab, cft, dt, vt)


def one_hot(shape, rows_per, cols_per):
    r = lax.broadcasted_iota(jnp.int32, shape, 0)
    c = lax.broadcasted_iota(jnp.int32, shape, 1)
    return r // rows_per == c // cols_per


def grams_of(own, got, rft, cft, keep, send, spread, unfold, rowbuf, total):
    rows, cols = got.shape[0], cft.shape[1]
    pixels = got.shape[2]
    pairs = own // 2
    n_cube = pairs * cols
    n_part = own * SCAN_RANK
    group = 16
    tall = one_hot((SCAN_RANK * group, SCAN_RANK), group, 1).astype(BF16)
    wide = one_hot((rows, rows * group), 1, group).astype(BF16)
    weights = dot(tall, rft[...]).astype(BF16)
    weights = dot(weights, wide)
    r = lax.broadcasted_iota(jnp.int32, weights.shape, 0)
    c = lax.broadcasted_iota(jnp.int32, weights.shape, 1)
    spread[...] = jnp.where(r % group == c % group, weights, 0.0).astype(BF16)

    def gather(start):
        return jnp.concatenate([got[s, pl.ds(start, group), :] for s in range(rows)], axis=0)

    for g in range(cols // group):
        x = jnp.concatenate([gather(h * cols + g * group) for h in range(pairs)], axis=1)
        u = dot(spread[...], x).astype(BF16)
        for i in range(SCAN_RANK):
            unfold[i, pl.ds(g * group, group), :] = u[i * group : (i + 1) * group]
    gram = jnp.zeros((cols, cols), F32)
    for i in range(SCAN_RANK):
        gram += dot(unfold[i], unfold[i], LAST)
    total[pl.ds(0, cols), :] = gram * SCAN_SCALE
    for s in range(rows):
        x = jnp.concatenate([got[s, pl.ds(h * cols, cols), :] for h in range(pairs)], axis=1)
        y = dot(cft[...], x)
        for h in range(pairs):
            rowbuf[h, pl.ds(s, SCAN_RANK, stride=rows), :] = y[:, h * LANES : (h + 1) * LANES]
    gram = jnp.zeros((rows, rows), F32)
    for i in range(SCAN_RANK):
        for h in range(pairs):
            x = rowbuf[h, pl.ds(i * rows, rows), :].astype(BF16)
            gram += dot(x, x, LAST)
    total[pl.ds(cols, rows), :] = jnp.zeros((rows, total.shape[1]), F32)
    total[pl.ds(cols, rows), pl.ds(0, rows)] = gram * SCAN_SCALE
    for side in range(2):
        gram = jnp.zeros((pixels, pixels), F32)
        for g in range(n_part // group):
            x = gather(n_cube + side * n_part + g * group)
            u = dot(spread[...], x).astype(BF16)
            gram += dot(u, u, FIRST)
        total[pl.ds(cols + rows + side * pixels, pixels), :] = gram * DET_SCALE
    half = keep.shape[0]
    core = lax.axis_index("row") % 2
    keep[...] = total[pl.ds(pl.multiple_of(core * half, 8), half), :]
    send[...] = total[pl.ds(pl.multiple_of((1 - core) * half, 8), half), :]


def partial_grams(own, got, rft, cft):
    rows, cols, pixels = rft.shape[1], cft.shape[1], got.shape[2]
    height = cols + rows + 2 * pixels
    half = jax.ShapeDtypeStruct((height // 2, pixels), F32)
    return pl.pallas_call(
        functools.partial(grams_of, own),
        out_shape=(half, half),
        scratch_shapes=[
            pltpu.VMEM((SCAN_RANK * 16, rows * 16), BF16),
            pltpu.VMEM((SCAN_RANK, cols, own * DET_RANK), BF16),
            pltpu.VMEM((own // 2, SCAN_RANK * rows, LANES), F32),
            pltpu.VMEM((height, pixels), F32),
        ],
        compiler_params=pltpu.CompilerParams(vmem_limit_bytes=40 << 20),
    )(got, rft, cft)


def swap(x, n, step):
    return lax.ppermute(x, "row", [(i, i ^ step) for i in range(n)])


def local(n, slab, row_factor, col_factor, det_row_factor, det_col_factor):
    slab = slab.reshape(slab.shape[-3:])
    cols, pixels = slab.shape[0], slab.shape[1]
    rows = row_factor.shape[0]
    own = DET_RANK // n
    packed = projections(n, (cols // 2, cols * 13 // 16), slab, col_factor.T, det_row_factor.T, det_col_factor.T)
    got = lax.all_to_all(packed, "row", split_axis=0, concat_axis=0, tiled=True)
    mine, other = partial_grams(own, got, row_factor.T, col_factor.T)
    mine = mine + swap(other, n, 1)
    step = 2
    while step < n:
        mine = mine + swap(mine, n, step)
        step *= 2
    other = swap(mine, n, 1)
    first = lax.axis_index("row") % 2 == 0
    grams = jnp.concatenate([jnp.where(first, mine, other), jnp.where(first, other, mine)])
    cut = cols + rows
    return (
        grams[cols:cut, :rows],
        grams[:cols],
        grams[cut : cut + pixels],
        grams[cut + pixels :],
    )


def all_sum(x, n):
    step = 1
    while step < n:
        x = x + swap(x, n, step)
        step *= 2
    return x


def plain(n, slab, row_factor, col_factor, det_row_factor, det_col_factor):
    slab = slab.reshape(slab.shape[-3:])
    rows, own = row_factor.shape[0], DET_RANK // n
    half_right = jnp.einsum("ckl,lb->cbk", slab, det_col_factor, preferred_element_type=F32).astype(BF16)
    half_left = jnp.einsum("ckl,ka->cal", slab, det_row_factor, preferred_element_type=F32).astype(BF16)
    cubes = jnp.einsum("cbk,ka->bca", half_right, det_row_factor, preferred_element_type=F32).astype(BF16)
    right_cols = jnp.einsum("cbk,cj->bjk", half_right, col_factor, preferred_element_type=F32).astype(BF16)
    left_cols = jnp.einsum("cal,cj->ajl", half_left, col_factor, preferred_element_type=F32).astype(BF16)
    cubes, right_cols, left_cols = (
        lax.all_to_all(x.reshape((n, own) + x.shape[1:]), "row", split_axis=0, concat_axis=0, tiled=True)
        for x in (cubes, right_cols, left_cols)
    )
    row_unfold = jnp.einsum("rbca,cj->rjba", cubes, col_factor, preferred_element_type=F32).astype(BF16)
    col_unfold = jnp.einsum("rbca,ri->ibca", cubes, row_factor, preferred_element_type=F32).astype(BF16)
    det_right = jnp.einsum("rbjk,ri->ibjk", right_cols, row_factor, preferred_element_type=F32).astype(BF16)
    det_left = jnp.einsum("rajl,ri->iajl", left_cols, row_factor, preferred_element_type=F32).astype(BF16)
    row_gram = jnp.einsum("rjba,sjba->rs", row_unfold, row_unfold, preferred_element_type=F32)
    col_gram = jnp.einsum("ibca,ibda->cd", col_unfold, col_unfold, preferred_element_type=F32)
    right_gram = jnp.einsum("ibjk,ibjm->km", det_right, det_right, preferred_element_type=F32)
    left_gram = jnp.einsum("iajl,iajm->lm", det_left, det_left, preferred_element_type=F32)
    scaled = (row_gram * SCAN_SCALE, col_gram * SCAN_SCALE, right_gram * DET_SCALE, left_gram * DET_SCALE)
    return lax.psum(scaled, "row")


def solution(mesh):
    in_specs = (
        P(("slab", "row"), None, None, None),
        P("slab", None),
        P("slab", None),
        P("slab", None),
        P("slab", None),
    )
    out_specs = (P("slab", None), P("slab", None), P("slab", None), P("slab", None))
    n = mesh.shape["row"]
    paired = DET_RANK % (2 * n) == 0 and n & (n - 1) == 0
    run = functools.partial(local if paired else plain, n)
    return jax.shard_map(run, mesh=mesh, in_specs=in_specs, out_specs=out_specs, check_vma=False)
```

```python
import functools

import jax
import jax.numpy as jnp
from jax import lax
from jax.experimental import pallas as pl
from jax.experimental.pallas import tpu as pltpu
from jax.sharding import PartitionSpec as P

DET_RANK = 64
SCAN_RANK = 8
SCAN_SCALE = 1.0 / (SCAN_RANK * DET_RANK * DET_RANK)
DET_SCALE = 1.0 / (SCAN_RANK * SCAN_RANK * DET_RANK)
LANES = 128
GROUP = 16
COST = pl.CostEstimate(flops=10**8, bytes_accessed=4 << 20, transcendentals=0)
BF16 = jnp.bfloat16
F32 = jnp.float32
LAST = (((1,), (1,)), ((), ()))
FIRST = (((0,), (0,)), ((), ()))


def dot(x, y, dims=None):
    if dims is None:
        return jnp.dot(x, y, preferred_element_type=F32)
    return lax.dot_general(x, y, dims, preferred_element_type=F32)


def paired(x):
    none = jnp.zeros_like(x)
    return jnp.concatenate([jnp.concatenate([x, none], 1), jnp.concatenate([none, x], 1)], 0)


def four_images(images, c):
    return jnp.concatenate(
        [
            jnp.concatenate([images[c], images[c + 1]], axis=1),
            jnp.concatenate([images[c + 2], images[c + 3]], axis=1),
        ],
        axis=0,
    )


def early_cubes(early, own, base, slab, dt_in, vt_in, *refs):
    *far, dd, dt, vt, images, right, arrived, ready = refs
    pixels = slab.shape[1]
    rank = own * far[0].shape[0] * len(far)
    pitch = early + 1
    cuts = [0, early // 2, early]
    copies = [
        pltpu.make_async_copy(slab.at[pl.ds(a, b - a)], images.at[pl.ds(a, b - a)], arrived.at[i])
        for i, (a, b) in enumerate(zip(cuts, cuts[1:]))
    ]
    factors = [pltpu.make_async_copy(x, y, ready.at[i]) for i, (x, y) in enumerate([(dt_in, dt), (vt_in, vt)])]
    for copy in factors + copies:
        copy.start()
    for copy in factors:
        copy.wait()
    vt2, dd[...] = paired(slot_order(vt[...], own, base, rank)), paired(dt[...].T)
    for at, copy in enumerate(copies):
        copy.wait()
        for c in range(cuts[at], cuts[at + 1], 4):
            rights = dot(vt2, four_images(images, c), LAST)
            for i in range(2):
                for j in range(2):
                    right[pl.ds(c + 2 * i + j, rank, stride=pitch), :] = rights[
                        j * rank : (j + 1) * rank, i * pixels : (i + 1) * pixels
                    ]
    owner_cubes(early, pitch, own, right, dd[...], far)


def slot_order(factor, own, base, count):
    shape = (count, factor.shape[0])
    r = lax.broadcasted_iota(jnp.int32, shape, 0) + base * own
    c = lax.broadcasted_iota(jnp.int32, shape, 1)
    take = (c // own == r // own ^ lax.axis_index("row")) & (c % own == r % own)
    return dot(take.astype(BF16), factor).astype(BF16)


def owner_cubes(early, pitch, own, right, dd, arrays):
    plane = arrays[0].shape[0]
    for slot in range(plane * len(arrays)):
        to = arrays[slot // plane].at[slot % plane]
        for h in range(own // 2):
            b = slot * own + 2 * h
            x = [right[pl.ds((b + k) * pitch, early), :] for k in range(2)]
            to[pl.ds(h * early, early), :] = dot(jnp.concatenate(x, axis=1).astype(BF16), dd).astype(BF16)


def late_cubes(early, own, images, cft, dt, vt, dd_in, *refs):
    *near, second, right, left, dd, ready = refs
    copy = pltpu.make_async_copy(dd_in, dd, ready)
    copy.start()
    cols, pixels, rank = images.shape[0], images.shape[1], dt.shape[0]
    pitch = cols + 1
    dt2, vt2 = (paired(slot_order(x[...], own, 0, rank)) for x in (dt, vt))
    for c in range(0, cols, 4):
        four = four_images(images, c)
        rights = dot(vt2, four, LAST)
        lefts = dot(dt2, four)
        for i in range(2):
            for j in range(2):
                at_c = pl.ds(c + 2 * i + j, rank, stride=pitch)
                right[at_c, :] = rights[j * rank : (j + 1) * rank, i * pixels : (i + 1) * pixels]
                left[at_c, :] = lefts[i * rank : (i + 1) * rank, j * pixels : (j + 1) * pixels]
    copy.wait()
    pairs, pair = own // 2, 2 * SCAN_RANK
    late = cols - early

    def two(ref, b):
        parts = [ref[pl.ds((b + k) * pitch, cols), :] for k in range(2)]
        return jnp.concatenate(parts, axis=1).astype(BF16)

    def stacked(sums):
        return jnp.concatenate([sums[:, :pixels], sums[:, pixels:]], axis=0).astype(BF16)

    me = lax.axis_index("row")
    for slot in range(rank // own):
        p = me ^ slot
        for h in range(pairs):
            x = two(right, slot * own + 2 * h)
            y = two(left, slot * own + 2 * h)
            at = pairs * late + h * pair
            second[p, pl.ds(h * late, late), :] = dot(x[early:], dd[...]).astype(BF16)
            second[p, pl.ds(at, pair), :] = stacked(dot(cft[...], x))
            second[p, pl.ds(at + pairs * pair, pair), :] = stacked(dot(cft[...], y))
    owner_cubes(early, pitch, own, right, dd[...], near)


def projections(n, plane, early, slab, cft, dt, vt):
    cols, pixels = slab.shape[0], slab.shape[1]
    rank = dt.shape[0]
    own = rank // n
    anywhere = pl.BlockSpec(memory_space=pl.ANY)
    in_vmem = pl.BlockSpec(memory_space=pltpu.VMEM)
    params = pltpu.CompilerParams(vmem_limit_bytes=56 << 20)
    half = n // plane // 2
    part = [jax.ShapeDtypeStruct((plane, own // 2 * early, pixels), BF16)] * half
    pair = jax.ShapeDtypeStruct((2 * pixels, 2 * rank), BF16)
    *far, dd = pl.pallas_call(
        functools.partial(early_cubes, early, own, n // 2),
        out_shape=part + [pair],
        in_specs=[anywhere] * 3,
        out_specs=[in_vmem] * (half + 1),
        scratch_shapes=[
            pltpu.VMEM(dt.shape, BF16),
            pltpu.VMEM(vt.shape, BF16),
            pltpu.VMEM((early,) + slab.shape[1:], BF16),
            pltpu.VMEM((rank // 2 * (early + 1), pixels), F32),
            pltpu.SemaphoreType.DMA((2,)),
            pltpu.SemaphoreType.DMA((2,)),
        ],
        compiler_params=params,
    )(slab, dt, vt)
    height = own // 2 * (cols - early) + 2 * own * SCAN_RANK
    *near, second = pl.pallas_call(
        functools.partial(late_cubes, early, own),
        out_shape=part + [jax.ShapeDtypeStruct((n, height, pixels), BF16)],
        in_specs=[in_vmem] * 4 + [anywhere],
        out_specs=[in_vmem] * (half + 1),
        scratch_shapes=[pltpu.VMEM((rank * (cols + 1), pixels), F32)] * 2
        + [pltpu.VMEM(dd.shape, BF16), pltpu.SemaphoreType.DMA],
        compiler_params=pltpu.CompilerParams(vmem_limit_bytes=32 << 20),
    )(slab, cft, dt, vt, dd)
    return near + far, second


def one_hot(shape, rows_per, cols_per):
    r = lax.broadcasted_iota(jnp.int32, shape, 0)
    c = lax.broadcasted_iota(jnp.int32, shape, 1)
    return r // rows_per == c // cols_per


def spread_weights(rft, rows, order=None):
    weights = rft[...]
    if order is not None:
        r = lax.broadcasted_iota(jnp.int32, (rows, rows), 0)
        c = lax.broadcasted_iota(jnp.int32, (rows, rows), 1)
        weights = dot(weights, (r == (c ^ order)).astype(BF16)).astype(BF16)
    tall = one_hot((SCAN_RANK * GROUP, SCAN_RANK), GROUP, 1).astype(BF16)
    wide = one_hot((rows, rows * GROUP), 1, GROUP).astype(BF16)
    weights = dot(dot(tall, weights).astype(BF16), wide)
    r = lax.broadcasted_iota(jnp.int32, weights.shape, 0)
    c = lax.broadcasted_iota(jnp.int32, weights.shape, 1)
    return jnp.where(r % GROUP == c % GROUP, weights, 0.0).astype(BF16)


def partial_grams(own, plane, early, rft, cft, second, *refs):
    *first, keep, send, unfold, rowbuf, total = refs
    rows, cols, pixels = rft.shape[1], cft.shape[1], second.shape[2]
    pairs, late = own // 2, cols - early
    me = lax.axis_index("row")
    mixed = spread_weights(rft, rows, me)
    plain = spread_weights(rft, rows)

    def old(s, at, size):
        return first[s % plane][s // plane, pl.ds(at, size), :]

    def new(s, at, size):
        return second[s, pl.ds(at, size), :]

    def wide(get, at, size, pitch):
        return jnp.concatenate([get(at + h * pitch, size) for h in range(pairs)], axis=1)

    def all_rows(get, at, size):
        return jnp.concatenate([get(s, at, size) for s in range(rows)], axis=0)

    for c in range(0, cols, GROUP):
        if c < early:
            u = dot(mixed, wide(functools.partial(all_rows, old), c, GROUP, early))
        else:
            u = dot(plain, wide(functools.partial(all_rows, new), c - early, GROUP, late))
        u = u.astype(BF16)
        for i in range(SCAN_RANK):
            unfold[i, pl.ds(c, GROUP), :] = u[i * GROUP : (i + 1) * GROUP]
    gram = jnp.zeros((cols, cols), F32)
    for i in range(SCAN_RANK):
        gram += dot(unfold[i], unfold[i], LAST)
    half = cols // 2
    pack(total, 0, gram * SCAN_SCALE)
    for s in range(rows):
        y = dot(cft[:, :early], wide(functools.partial(old, s), 0, early, early))
        z = dot(cft[:, early:], wide(functools.partial(new, s), 0, late, late))
        for h in range(pairs):
            lanes = slice(h * LANES, (h + 1) * LANES)
            rowbuf[0, h, pl.ds(me ^ s, SCAN_RANK, stride=rows), :] = y[:, lanes]
            rowbuf[1, h, pl.ds(s, SCAN_RANK, stride=rows), :] = z[:, lanes]
    gram = jnp.zeros((rows, rows), F32)
    for i in range(SCAN_RANK):
        for h in range(pairs):
            at = pl.ds(i * rows, rows)
            x = (rowbuf[0, h, at, :] + rowbuf[1, h, at, :]).astype(BF16)
            gram += dot(x, x, LAST)
    spare = jnp.concatenate([gram * SCAN_SCALE, jnp.zeros((rows, half - rows), F32)], axis=1)
    total[pl.ds(5 * half - rows, rows), pl.ds(half, half)] = spare
    n_part = own * SCAN_RANK
    for side in range(2):
        gram = jnp.zeros((pixels, pixels), F32)
        for g in range(n_part // GROUP):
            at = pairs * late + side * n_part + g * GROUP
            u = dot(plain, all_rows(new, at, GROUP)).astype(BF16)
            gram += dot(u, u, FIRST)
        pack(total, 1 + side, gram * DET_SCALE)
    size = keep.shape[0]
    core = me % 2
    keep[...] = total[pl.ds(pl.multiple_of(core * size, 8), size), :]
    send[...] = total[pl.ds(pl.multiple_of((1 - core) * size, 8), size), :]


def pack(total, k, gram):
    half = gram.shape[0] // 2
    total[pl.ds(k * half, half), :] = gram[:half]
    total[pl.ds((3 + k // 2) * half, half), pl.ds(k % 2 * half, half)] = gram[half:, half:]


def unpack(mine, other, row_out, col_out, right_out, left_out, row_gram, grams, sems):
    even = lax.axis_index("row") % 2 == 0
    total = jnp.concatenate(
        [jnp.where(even, mine[...], other[...]), jnp.where(even, other[...], mine[...])], axis=0
    )
    cols, rows = col_out.shape[0], row_out.shape[0]
    half = cols // 2
    copies = []
    for k, out in enumerate([col_out, right_out, left_out]):
        top = total[k * half : (k + 1) * half]
        corner = total[(3 + k // 2) * half : (4 + k // 2) * half, k % 2 * half : (k % 2 + 1) * half]
        grams[k, pl.ds(0, half), :] = top
        grams[k, pl.ds(half, half), :] = jnp.concatenate([top[:, half:].T, corner], axis=1)
        copies.append(pltpu.make_async_copy(grams.at[k], out, sems.at[k]))
        copies[-1].start()
    row_gram[...] = total[5 * half - rows : 5 * half, half : half + rows]
    copies.append(pltpu.make_async_copy(row_gram, row_out, sems.at[3]))
    copies[-1].start()
    for copy in copies:
        copy.wait()


def call(kernel, args, outs, scratch=(), flops=10**8):
    return pl.pallas_call(
        kernel,
        out_shape=[jax.ShapeDtypeStruct(shape, F32) for shape in outs],
        scratch_shapes=scratch,
        compiler_params=pltpu.CompilerParams(vmem_limit_bytes=40 << 20),
        cost_estimate=pl.CostEstimate(flops=flops, bytes_accessed=4 << 20, transcendentals=0),
    )(*args)


def swap(x, n, step):
    return lax.ppermute(x, "row", [(i, i ^ step) for i in range(n)])


def regroup(*refs):
    before, after = refs[: len(refs) // 2], refs[len(refs) // 2 :]
    for z, x in enumerate(before):
        for q, y in enumerate(after):
            y[z] = x[q]


def regrouped(first):
    planes, (plane, height, width) = len(first), first[0].shape
    return pl.pallas_call(
        regroup,
        out_shape=[jax.ShapeDtypeStruct((planes, height, width), BF16)] * plane,
        compiler_params=pltpu.CompilerParams(vmem_limit_bytes=40 << 20),
        cost_estimate=pl.CostEstimate(flops=4 * 10**10, bytes_accessed=4 << 20, transcendentals=0),
    )(*first)


def all_sum(mine, other, n):
    mine = mine + swap(other, n, 1)
    step = 2
    while step < n:
        mine = mine + swap(mine, n, step)
        step *= 2
    return mine, swap(mine, n, 1)


def local(n, plane, slab, row_factor, col_factor, det_row_factor, det_col_factor):
    slab = slab.reshape(slab.shape[-3:])
    cols, pixels = slab.shape[0], slab.shape[1]
    rows = row_factor.shape[0]
    own = DET_RANK // n
    rft, cft = row_factor.T, col_factor.T
    early = cols // 2
    first, second = projections(n, plane, early, slab, cft, det_row_factor.T, det_col_factor.T)
    first = [x if z == 0 else swap(x, n, z * plane) for z, x in enumerate(first)]
    second = lax.all_to_all(second, "row", split_axis=0, concat_axis=0, tiled=True)
    first = regrouped(first)
    first = [x if q == 0 else swap(x, n, q) for q, x in enumerate(first)]
    half = (5 * cols // 4, pixels)
    scratch = [
        pltpu.VMEM((SCAN_RANK, cols, own * DET_RANK), BF16),
        pltpu.VMEM((2, own // 2, SCAN_RANK * rows, LANES), F32),
        pltpu.VMEM((5 * cols // 2, pixels), F32),
    ]
    kernel = functools.partial(partial_grams, own, plane, early)
    mine, other = call(kernel, (rft, cft, second, *first), (half, half), scratch)
    mine, other = all_sum(mine, other, n)
    outs = [(rows, rows), (cols, cols), (pixels, pixels), (pixels, pixels)]
    in_vmem = pl.BlockSpec(memory_space=pltpu.VMEM)
    return pl.pallas_call(
        unpack,
        out_shape=[jax.ShapeDtypeStruct(shape, F32) for shape in outs],
        in_specs=[in_vmem] * 2,
        out_specs=[pl.BlockSpec(memory_space=pl.ANY)] * 4,
        scratch_shapes=[
            pltpu.VMEM((rows, rows), F32),
            pltpu.VMEM((3, cols, cols), F32),
            pltpu.SemaphoreType.DMA((4,)),
        ],
    )(mine, other)


def plain(n, slab, row_factor, col_factor, det_row_factor, det_col_factor):
    slab = slab.reshape(slab.shape[-3:])
    rows, own = row_factor.shape[0], DET_RANK // n
    half_right = jnp.einsum("ckl,lb->cbk", slab, det_col_factor, preferred_element_type=F32).astype(BF16)
    half_left = jnp.einsum("ckl,ka->cal", slab, det_row_factor, preferred_element_type=F32).astype(BF16)
    cubes = jnp.einsum("cbk,ka->bca", half_right, det_row_factor, preferred_element_type=F32).astype(BF16)
    right_cols = jnp.einsum("cbk,cj->bjk", half_right, col_factor, preferred_element_type=F32).astype(BF16)
    left_cols = jnp.einsum("cal,cj->ajl", half_left, col_factor, preferred_element_type=F32).astype(BF16)
    cubes, right_cols, left_cols = (
        lax.all_to_all(x.reshape((n, own) + x.shape[1:]), "row", split_axis=0, concat_axis=0, tiled=True)
        for x in (cubes, right_cols, left_cols)
    )
    row_unfold = jnp.einsum("rbca,cj->rjba", cubes, col_factor, preferred_element_type=F32).astype(BF16)
    col_unfold = jnp.einsum("rbca,ri->ibca", cubes, row_factor, preferred_element_type=F32).astype(BF16)
    det_right = jnp.einsum("rbjk,ri->ibjk", right_cols, row_factor, preferred_element_type=F32).astype(BF16)
    det_left = jnp.einsum("rajl,ri->iajl", left_cols, row_factor, preferred_element_type=F32).astype(BF16)
    row_gram = jnp.einsum("rjba,sjba->rs", row_unfold, row_unfold, preferred_element_type=F32)
    col_gram = jnp.einsum("ibca,ibda->cd", col_unfold, col_unfold, preferred_element_type=F32)
    right_gram = jnp.einsum("ibjk,ibjm->km", det_right, det_right, preferred_element_type=F32)
    left_gram = jnp.einsum("iajl,iajm->lm", det_left, det_left, preferred_element_type=F32)
    scaled = (row_gram * SCAN_SCALE, col_gram * SCAN_SCALE, right_gram * DET_SCALE, left_gram * DET_SCALE)
    return lax.psum(scaled, "row")


def solution(mesh):
    in_specs = (
        P(("slab", "row"), None, None, None),
        P("slab", None),
        P("slab", None),
        P("slab", None),
        P("slab", None),
    )
    out_specs = (P("slab", None), P("slab", None), P("slab", None), P("slab", None))
    n = mesh.shape["row"]
    plane = round(n**0.5)
    tuned = plane * plane == n and n & (n - 1) == 0 and DET_RANK % (2 * n) == 0
    run = functools.partial(local, n, plane) if tuned else functools.partial(plain, n)
    return jax.shard_map(run, mesh=mesh, in_specs=in_specs, out_specs=out_specs, check_vma=False)
```

```python
import functools

import jax
import jax.numpy as jnp
from jax import lax
from jax.experimental import pallas as pl
from jax.experimental.pallas import tpu as pltpu
from jax.sharding import PartitionSpec as P

DET_RANK = 64
SCAN_RANK = 8
SCAN_SCALE = 1.0 / (SCAN_RANK * DET_RANK * DET_RANK)
DET_SCALE = 1.0 / (SCAN_RANK * SCAN_RANK * DET_RANK)
LANES = 128
GROUP = 16
BF16 = jnp.bfloat16
F32 = jnp.float32
LAST = (((1,), (1,)), ((), ()))
FIRST = (((0,), (0,)), ((), ()))


def dot(x, y, dims=None):
    if dims is None:
        return jnp.dot(x, y, preferred_element_type=F32)
    return lax.dot_general(x, y, dims, preferred_element_type=F32)


def paired(x):
    none = jnp.zeros_like(x)
    return jnp.concatenate([jnp.concatenate([x, none], 1), jnp.concatenate([none, x], 1)], 0)


def four_images(images, c):
    return jnp.concatenate(
        [
            jnp.concatenate([images[c], images[c + 1]], axis=1),
            jnp.concatenate([images[c + 2], images[c + 3]], axis=1),
        ],
        axis=0,
    )


def early_cubes(early, own, base, slab, dt_in, vt_in, *refs):
    *outs, dt, vt, images, right, far, arrived, ready, sent = refs
    pixels = slab.shape[1]
    plane = outs[0].shape[0]
    rank = own * plane * len(outs)
    pitch = early + 1
    cuts = [0, early // 2, early]
    copies = [
        pltpu.make_async_copy(slab.at[pl.ds(a, b - a)], images.at[pl.ds(a, b - a)], arrived.at[i])
        for i, (a, b) in enumerate(zip(cuts, cuts[1:]))
    ]
    factors = [pltpu.make_async_copy(x, y, ready.at[i]) for i, (x, y) in enumerate([(dt_in, dt), (vt_in, vt)])]
    for copy in factors + copies:
        copy.start()
    for copy in factors:
        copy.wait()
    vt2, dd = paired(slot_order(vt[...], own, base, rank)), paired(dt[...].T)
    for at, copy in enumerate(copies):
        copy.wait()
        for c in range(cuts[at], cuts[at + 1], 4):
            rights = dot(vt2, four_images(images, c), LAST)
            for i in range(2):
                for j in range(2):
                    right[pl.ds(c + 2 * i + j, rank, stride=pitch), :] = rights[
                        j * rank : (j + 1) * rank, i * pixels : (i + 1) * pixels
                    ]
    copies = []
    for slot in range(plane * len(outs)):
        slot_cubes(slot, early, pitch, own, right, dd, far.at[slot])
        out = outs[slot // plane].at[slot % plane]
        copies.append(pltpu.make_async_copy(far.at[slot], out, sent.at[slot]))
        copies[-1].start()
    for copy in copies:
        copy.wait()


def slot_order(factor, own, base, count):
    shape = (count, factor.shape[0])
    r = lax.broadcasted_iota(jnp.int32, shape, 0) + base * own
    c = lax.broadcasted_iota(jnp.int32, shape, 1)
    take = (c // own == r // own ^ lax.axis_index("row")) & (c % own == r % own)
    return dot(take.astype(BF16), factor).astype(BF16)


def slot_cubes(slot, early, pitch, own, right, dd, to):
    for h in range(own // 2):
        b = slot * own + 2 * h
        x = [right[pl.ds((b + k) * pitch, early), :] for k in range(2)]
        to[pl.ds(h * early, early), :] = dot(jnp.concatenate(x, axis=1).astype(BF16), dd).astype(BF16)


def late_cubes(early, own, images, cft, dt, vt, *refs):
    *near, out, right, left, second, sent = refs
    cols, pixels, rank = images.shape[0], images.shape[1], dt.shape[0]
    pitch = cols + 1
    dt2, vt2 = (paired(slot_order(x[...], own, 0, rank)) for x in (dt, vt))
    for c in range(0, cols, 4):
        four = four_images(images, c)
        rights = dot(vt2, four, LAST)
        lefts = dot(dt2, four)
        for i in range(2):
            for j in range(2):
                at_c = pl.ds(c + 2 * i + j, rank, stride=pitch)
                right[at_c, :] = rights[j * rank : (j + 1) * rank, i * pixels : (i + 1) * pixels]
                left[at_c, :] = lefts[i * rank : (i + 1) * rank, j * pixels : (j + 1) * pixels]
    dd = paired(dt[...].T)
    pairs, pair = own // 2, 2 * SCAN_RANK
    late = cols - early

    def two(ref, b):
        parts = [ref[pl.ds((b + k) * pitch, cols), :] for k in range(2)]
        return jnp.concatenate(parts, axis=1).astype(BF16)

    def stacked(sums):
        return jnp.concatenate([sums[:, :pixels], sums[:, pixels:]], axis=0).astype(BF16)

    me = lax.axis_index("row")
    copies = []
    for slot in range(rank // own):
        p = me ^ slot
        for h in range(pairs):
            x = two(right, slot * own + 2 * h)
            y = two(left, slot * own + 2 * h)
            at = pairs * late + h * pair
            second[slot, pl.ds(h * late, late), :] = dot(x[early:], dd).astype(BF16)
            second[slot, pl.ds(at, pair), :] = stacked(dot(cft[...], x))
            second[slot, pl.ds(at + pairs * pair, pair), :] = stacked(dot(cft[...], y))
        copies.append(pltpu.make_async_copy(second.at[slot], out.at[p], sent.at[slot]))
        copies[-1].start()
    plane = near[0].shape[0]
    for slot in range(plane * len(near)):
        slot_cubes(slot, early, pitch, own, right, dd, near[slot // plane].at[slot % plane])
    for copy in copies:
        copy.wait()


def projections(n, plane, early, slab, cft, dt, vt):
    cols, pixels = slab.shape[0], slab.shape[1]
    rank = dt.shape[0]
    own = rank // n
    anywhere = pl.BlockSpec(memory_space=pl.ANY)
    in_vmem = pl.BlockSpec(memory_space=pltpu.VMEM)
    params = pltpu.CompilerParams(vmem_limit_bytes=56 << 20)
    half = n // plane // 2
    part = [jax.ShapeDtypeStruct((plane, own // 2 * early, pixels), BF16)] * half
    far = pl.pallas_call(
        functools.partial(early_cubes, early, own, n // 2),
        out_shape=part,
        in_specs=[anywhere] * 3,
        out_specs=[anywhere] * half,
        scratch_shapes=[
            pltpu.VMEM(dt.shape, BF16),
            pltpu.VMEM(vt.shape, BF16),
            pltpu.VMEM((early,) + slab.shape[1:], BF16),
            pltpu.VMEM((rank // 2 * (early + 1), pixels), F32),
            pltpu.VMEM((n // 2, own // 2 * early, pixels), BF16),
            pltpu.SemaphoreType.DMA((2,)),
            pltpu.SemaphoreType.DMA((2,)),
            pltpu.SemaphoreType.DMA((n // 2,)),
        ],
        compiler_params=params,
    )(slab, dt, vt)
    height = own // 2 * (cols - early) + 2 * own * SCAN_RANK
    *near, second = pl.pallas_call(
        functools.partial(late_cubes, early, own),
        out_shape=part + [jax.ShapeDtypeStruct((n, height, pixels), BF16)],
        in_specs=[in_vmem] * 4,
        out_specs=[in_vmem] * half + [anywhere],
        scratch_shapes=[pltpu.VMEM((rank * (cols + 1), pixels), F32)] * 2
        + [pltpu.VMEM((n, height, pixels), BF16), pltpu.SemaphoreType.DMA((n,))],
        compiler_params=pltpu.CompilerParams(vmem_limit_bytes=32 << 20),
    )(slab, cft, dt, vt)
    return near + list(far), second


def one_hot(shape, rows_per, cols_per):
    r = lax.broadcasted_iota(jnp.int32, shape, 0)
    c = lax.broadcasted_iota(jnp.int32, shape, 1)
    return r // rows_per == c // cols_per


def spread_weights(rft, rows, order=None):
    weights = rft[...]
    if order is not None:
        r = lax.broadcasted_iota(jnp.int32, (rows, rows), 0)
        c = lax.broadcasted_iota(jnp.int32, (rows, rows), 1)
        weights = dot(weights, (r == (c ^ order)).astype(BF16)).astype(BF16)
    tall = one_hot((SCAN_RANK * GROUP, SCAN_RANK), GROUP, 1).astype(BF16)
    wide = one_hot((rows, rows * GROUP), 1, GROUP).astype(BF16)
    weights = dot(dot(tall, weights).astype(BF16), wide)
    r = lax.broadcasted_iota(jnp.int32, weights.shape, 0)
    c = lax.broadcasted_iota(jnp.int32, weights.shape, 1)
    return jnp.where(r % GROUP == c % GROUP, weights, 0.0).astype(BF16)


def wide(get, at, size, pitch, pairs):
    return jnp.concatenate([get(at + h * pitch, size) for h in range(pairs)], axis=1)


def stack_rows(arrays, at, size):
    return jnp.concatenate([x[pl.ds(at, size), :] for x in arrays], axis=0)


def store_unfold(unfold, at, u):
    for i in range(SCAN_RANK):
        unfold[i, pl.ds(at, GROUP), :] = u[i * GROUP : (i + 1) * GROUP]


def early_grams(own, plane, rft, cft, *refs):
    *first, plain, unfold, rowpart, corner = refs
    rows = rft.shape[1]
    pairs = own // 2
    early = first[0].shape[1] // pairs
    me = lax.axis_index("row")
    mixed = spread_weights(rft, rows, me)
    plain[...] = spread_weights(rft, rows)
    slots = [first[s % plane].at[s // plane] for s in range(rows)]
    for c in range(0, early, GROUP):
        x = wide(functools.partial(stack_rows, slots), c, GROUP, early, pairs)
        store_unfold(unfold, c, dot(mixed, x).astype(BF16))
    gram = jnp.zeros((early, early), F32)
    for i in range(SCAN_RANK):
        gram += dot(unfold[i], unfold[i], LAST)
    corner[...] = gram * SCAN_SCALE
    for s in range(rows):
        x = wide(lambda at, size: slots[s][pl.ds(at, size), :], 0, early, early, pairs)
        y = dot(cft[:, :early], x)
        for h in range(pairs):
            rowpart[h, pl.ds(me ^ s, SCAN_RANK, stride=rows), :] = y[:, h * LANES : (h + 1) * LANES]


def partial_grams(own, cft, plain, early_unfold, rowpart, corner, second, keep, send, unfold, rowbuf, total):
    rows, cols, pixels = second.shape[0], cft.shape[1], second.shape[2]
    pairs, half = own // 2, cols // 2
    slots = [second.at[s] for s in range(rows)]
    for c in range(0, half, GROUP):
        x = wide(functools.partial(stack_rows, slots), c, GROUP, half, pairs)
        store_unfold(unfold, c, dot(plain[...], x).astype(BF16))
    side = jnp.zeros((half, half), F32)
    gram = jnp.zeros((half, half), F32)
    for i in range(SCAN_RANK):
        side += dot(early_unfold[i], unfold[i], LAST)
        gram += dot(unfold[i], unfold[i], LAST)
    total[pl.ds(0, half), :] = jnp.concatenate([corner[...], side * SCAN_SCALE], axis=1)
    total[pl.ds(3 * half, half), pl.ds(0, half)] = gram * SCAN_SCALE
    for s in range(rows):
        x = wide(lambda at, size: slots[s][pl.ds(at, size), :], 0, half, half, pairs)
        y = dot(cft[:, half:], x)
        for h in range(pairs):
            rowbuf[h, pl.ds(s, SCAN_RANK, stride=rows), :] = y[:, h * LANES : (h + 1) * LANES]
    gram = jnp.zeros((rows, rows), F32)
    for i in range(SCAN_RANK):
        for h in range(pairs):
            at = pl.ds(i * rows, rows)
            x = (rowbuf[h, at, :] + rowpart[h, at, :]).astype(BF16)
            gram += dot(x, x, LAST)
    spare = jnp.concatenate([gram * SCAN_SCALE, jnp.zeros((rows, half - rows), F32)], axis=1)
    total[pl.ds(5 * half - rows, rows), pl.ds(half, half)] = spare
    n_part = own * SCAN_RANK
    for k in range(2):
        gram = jnp.zeros((pixels, pixels), F32)
        for g in range(n_part // GROUP):
            at = pairs * half + k * n_part + g * GROUP
            u = dot(plain[...], stack_rows(slots, at, GROUP)).astype(BF16)
            gram += dot(u, u, FIRST)
        gram *= DET_SCALE
        total[pl.ds((1 + k) * half, half), :] = gram[:half]
        total[pl.ds((3 + (1 + k) // 2) * half, half), pl.ds((1 + k) % 2 * half, half)] = gram[half:, half:]
    size = keep.shape[0]
    core = lax.axis_index("row") % 2
    keep[...] = total[pl.ds(pl.multiple_of(core * size, 8), size), :]
    send[...] = total[pl.ds(pl.multiple_of((1 - core) * size, 8), size), :]


def unpack(mine, other, row_out, col_out, right_out, left_out, row_gram, grams, sems):
    even = lax.axis_index("row") % 2 == 0
    total = jnp.concatenate(
        [jnp.where(even, mine[...], other[...]), jnp.where(even, other[...], mine[...])], axis=0
    )
    cols, rows = col_out.shape[0], row_out.shape[0]
    half = cols // 2
    copies = []
    for k, out in enumerate([col_out, right_out, left_out]):
        top = total[k * half : (k + 1) * half]
        corner = total[(3 + k // 2) * half : (4 + k // 2) * half, k % 2 * half : (k % 2 + 1) * half]
        grams[k, pl.ds(0, half), :] = top
        grams[k, pl.ds(half, half), :] = jnp.concatenate([top[:, half:].T, corner], axis=1)
        copies.append(pltpu.make_async_copy(grams.at[k], out, sems.at[k]))
        copies[-1].start()
    row_gram[...] = total[5 * half - rows : 5 * half, half : half + rows]
    copies.append(pltpu.make_async_copy(row_gram, row_out, sems.at[3]))
    copies[-1].start()
    for copy in copies:
        copy.wait()


def call(kernel, args, outs, scratch=(), cost=10**8):
    return pl.pallas_call(
        kernel,
        out_shape=[jax.ShapeDtypeStruct(*out) for out in outs],
        scratch_shapes=scratch,
        compiler_params=pltpu.CompilerParams(vmem_limit_bytes=40 << 20),
        cost_estimate=pl.CostEstimate(flops=cost, bytes_accessed=1 << 20, transcendentals=0),
    )(*args)


def swap(x, n, step):
    return lax.ppermute(x, "row", [(i, i ^ step) for i in range(n)])


def by_place(plane, *refs):
    before, after = refs[:-plane], refs[-plane:]
    for z, x in enumerate(before):
        for q, y in enumerate(after):
            y[z] = x[q]


def join_planes(near, *refs):
    plane = (len(refs) - near) // 2
    before, far, after = refs[:near], refs[near : near + plane], refs[near + plane :]
    for q, y in enumerate(after):
        for z, x in enumerate(before):
            y[z] = x[q]
        y[pl.ds(near, y.shape[0] - near)] = far[q][...]


def regrouped(near, far):
    plane, height, width = near[0].shape
    some = [((len(far), height, width), BF16)] * plane
    every = [((len(near) + len(far), height, width), BF16)] * plane
    far = call(functools.partial(by_place, plane), far, some, cost=4 * 10**10)
    return call(functools.partial(join_planes, len(near)), (*near, *far), every)


def all_sum(mine, other, n):
    mine = mine + swap(other, n, 1)
    step = 2
    while step < n:
        mine = mine + swap(mine, n, step)
        step *= 2
    return mine, swap(mine, n, 1)


def local(n, plane, slab, row_factor, col_factor, det_row_factor, det_col_factor):
    slab = slab.reshape(slab.shape[-3:])
    cols, pixels = slab.shape[0], slab.shape[1]
    rows = row_factor.shape[0]
    own = DET_RANK // n
    rft, cft = row_factor.T, col_factor.T
    early = cols // 2
    first, second = projections(n, plane, early, slab, cft, det_row_factor.T, det_col_factor.T)
    first = [x if z == 0 else swap(x, n, z * plane) for z, x in enumerate(first)]
    second = lax.all_to_all(second, "row", split_axis=0, concat_axis=0, tiled=True)
    first = regrouped(first[: plane // 2], first[plane // 2 :])
    first = [x if q == 0 else swap(x, n, q) for q, x in enumerate(first)]
    pairs, width = own // 2, own * DET_RANK
    row_shape = (pairs, SCAN_RANK * rows, LANES)
    shapes = [
        ((SCAN_RANK * GROUP, rows * GROUP), BF16),
        ((SCAN_RANK, early, width), BF16),
        (row_shape, F32),
        ((early, early), F32),
    ]
    known = call(functools.partial(early_grams, own, plane), (rft, cft, *first), shapes)
    scratch = [
        pltpu.VMEM((SCAN_RANK, early, width), BF16),
        pltpu.VMEM(row_shape, F32),
        pltpu.VMEM((5 * cols // 2, pixels), F32),
    ]
    mine, other = call(
        functools.partial(partial_grams, own), (cft, *known, second), [((5 * cols // 4, pixels), F32)] * 2, scratch
    )
    mine, other = all_sum(mine, other, n)
    outs = [(rows, rows), (cols, cols), (pixels, pixels), (pixels, pixels)]
    in_vmem = pl.BlockSpec(memory_space=pltpu.VMEM)
    return pl.pallas_call(
        unpack,
        out_shape=[jax.ShapeDtypeStruct(shape, F32) for shape in outs],
        in_specs=[in_vmem] * 2,
        out_specs=[pl.BlockSpec(memory_space=pl.ANY)] * 4,
        scratch_shapes=[
            pltpu.VMEM((rows, rows), F32),
            pltpu.VMEM((3, cols, cols), F32),
            pltpu.SemaphoreType.DMA((4,)),
        ],
        compiler_params=pltpu.CompilerParams(vmem_limit_bytes=16 << 20),
    )(mine, other)


def plain(n, slab, row_factor, col_factor, det_row_factor, det_col_factor):
    slab = slab.reshape(slab.shape[-3:])
    rows, own = row_factor.shape[0], DET_RANK // n
    half_right = jnp.einsum("ckl,lb->cbk", slab, det_col_factor, preferred_element_type=F32).astype(BF16)
    half_left = jnp.einsum("ckl,ka->cal", slab, det_row_factor, preferred_element_type=F32).astype(BF16)
    cubes = jnp.einsum("cbk,ka->bca", half_right, det_row_factor, preferred_element_type=F32).astype(BF16)
    right_cols = jnp.einsum("cbk,cj->bjk", half_right, col_factor, preferred_element_type=F32).astype(BF16)
    left_cols = jnp.einsum("cal,cj->ajl", half_left, col_factor, preferred_element_type=F32).astype(BF16)
    cubes, right_cols, left_cols = (
        lax.all_to_all(x.reshape((n, own) + x.shape[1:]), "row", split_axis=0, concat_axis=0, tiled=True)
        for x in (cubes, right_cols, left_cols)
    )
    row_unfold = jnp.einsum("rbca,cj->rjba", cubes, col_factor, preferred_element_type=F32).astype(BF16)
    col_unfold = jnp.einsum("rbca,ri->ibca", cubes, row_factor, preferred_element_type=F32).astype(BF16)
    det_right = jnp.einsum("rbjk,ri->ibjk", right_cols, row_factor, preferred_element_type=F32).astype(BF16)
    det_left = jnp.einsum("rajl,ri->iajl", left_cols, row_factor, preferred_element_type=F32).astype(BF16)
    row_gram = jnp.einsum("rjba,sjba->rs", row_unfold, row_unfold, preferred_element_type=F32)
    col_gram = jnp.einsum("ibca,ibda->cd", col_unfold, col_unfold, preferred_element_type=F32)
    right_gram = jnp.einsum("ibjk,ibjm->km", det_right, det_right, preferred_element_type=F32)
    left_gram = jnp.einsum("iajl,iajm->lm", det_left, det_left, preferred_element_type=F32)
    scaled = (row_gram * SCAN_SCALE, col_gram * SCAN_SCALE, right_gram * DET_SCALE, left_gram * DET_SCALE)
    return lax.psum(scaled, "row")


def solution(mesh):
    in_specs = (
        P(("slab", "row"), None, None, None),
        P("slab", None),
        P("slab", None),
        P("slab", None),
        P("slab", None),
    )
    out_specs = (P("slab", None), P("slab", None), P("slab", None), P("slab", None))
    n = mesh.shape["row"]
    plane = round(n**0.5)
    tuned = plane * plane == n and n & (n - 1) == 0 and DET_RANK % (2 * n) == 0
    run = functools.partial(local, n, plane) if tuned else functools.partial(plain, n)
    return jax.shard_map(run, mesh=mesh, in_specs=in_specs, out_specs=out_specs, check_vma=False)
```

```python
import functools

import jax
import jax.numpy as jnp
from jax import lax
from jax.experimental import pallas as pl
from jax.experimental.pallas import tpu as pltpu
from jax.sharding import PartitionSpec as P

DET_RANK = 64
SCAN_RANK = 8
SCAN_SCALE = 1.0 / (SCAN_RANK * DET_RANK * DET_RANK)
DET_SCALE = 1.0 / (SCAN_RANK * SCAN_RANK * DET_RANK)
LANES = 128
GROUP = 16
BF16 = jnp.bfloat16
F32 = jnp.float32
LAST = (((1,), (1,)), ((), ()))
FIRST = (((0,), (0,)), ((), ()))


def dot(x, y, dims=None):
    if dims is None:
        return jnp.dot(x, y, preferred_element_type=F32)
    return lax.dot_general(x, y, dims, preferred_element_type=F32)


def paired(x):
    none = jnp.zeros_like(x)
    return jnp.concatenate([jnp.concatenate([x, none], 1), jnp.concatenate([none, x], 1)], 0)


def four_images(images, c):
    return jnp.concatenate(
        [
            jnp.concatenate([images[c], images[c + 1]], axis=1),
            jnp.concatenate([images[c + 2], images[c + 3]], axis=1),
        ],
        axis=0,
    )


def early_cubes(early, own, base, slab, dt_in, vt_in, *refs):
    *far, dt, vt, images, right, arrived, ready = refs
    pixels = slab.shape[1]
    plane = far[0].shape[0]
    rank = own * plane * len(far)
    pitch = early + 1
    cuts = [0, early // 2, early]
    copies = [
        pltpu.make_async_copy(slab.at[pl.ds(a, b - a)], images.at[pl.ds(a, b - a)], arrived.at[i])
        for i, (a, b) in enumerate(zip(cuts, cuts[1:]))
    ]
    factors = [pltpu.make_async_copy(x, y, ready.at[i]) for i, (x, y) in enumerate([(dt_in, dt), (vt_in, vt)])]
    for copy in factors + copies:
        copy.start()
    for copy in factors:
        copy.wait()
    vt2, dd = paired(slot_order(vt[...], own, base, rank)), paired(dt[...].T)
    for at, copy in enumerate(copies):
        copy.wait()
        for c in range(cuts[at], cuts[at + 1], 4):
            rights = dot(vt2, four_images(images, c), LAST)
            for i in range(2):
                for j in range(2):
                    right[pl.ds(c + 2 * i + j, rank, stride=pitch), :] = rights[
                        j * rank : (j + 1) * rank, i * pixels : (i + 1) * pixels
                    ]
    for slot in range(plane * len(far)):
        slot_cubes(slot, early, pitch, own, right, dd, far[slot // plane].at[slot % plane])


def slot_order(factor, own, base, count):
    shape = (count, factor.shape[0])
    r = lax.broadcasted_iota(jnp.int32, shape, 0) + base * own
    c = lax.broadcasted_iota(jnp.int32, shape, 1)
    take = (c // own == r // own ^ lax.axis_index("row")) & (c % own == r % own)
    return dot(take.astype(BF16), factor).astype(BF16)


def slot_cubes(slot, early, pitch, own, right, dd, to):
    for h in range(own // 2):
        b = slot * own + 2 * h
        x = [right[pl.ds((b + k) * pitch, early), :] for k in range(2)]
        to[pl.ds(h * early, early), :] = dot(jnp.concatenate(x, axis=1).astype(BF16), dd).astype(BF16)


def late_cubes(early, own, images, cft, dt, vt, *refs):
    *near, out, right, left, second, sent = refs
    cols, pixels, rank = images.shape[0], images.shape[1], dt.shape[0]
    pitch = cols + 1
    dt2, vt2 = (paired(slot_order(x[...], own, 0, rank)) for x in (dt, vt))
    for c in range(0, cols, 4):
        four = four_images(images, c)
        rights = dot(vt2, four, LAST)
        lefts = dot(dt2, four)
        for i in range(2):
            for j in range(2):
                at_c = pl.ds(c + 2 * i + j, rank, stride=pitch)
                right[at_c, :] = rights[j * rank : (j + 1) * rank, i * pixels : (i + 1) * pixels]
                left[at_c, :] = lefts[i * rank : (i + 1) * rank, j * pixels : (j + 1) * pixels]
    dd = paired(dt[...].T)
    pairs, pair = own // 2, 2 * SCAN_RANK
    late = cols - early

    def two(ref, b):
        parts = [ref[pl.ds((b + k) * pitch, cols), :] for k in range(2)]
        return jnp.concatenate(parts, axis=1).astype(BF16)

    def stacked(sums):
        return jnp.concatenate([sums[:, :pixels], sums[:, pixels:]], axis=0).astype(BF16)

    me = lax.axis_index("row")
    copies = []
    for slot in range(rank // own):
        p = me ^ slot
        for h in range(pairs):
            x = two(right, slot * own + 2 * h)
            y = two(left, slot * own + 2 * h)
            at = pairs * late + h * pair
            second[slot, pl.ds(h * late, late), :] = dot(x[early:], dd).astype(BF16)
            second[slot, pl.ds(at, pair), :] = stacked(dot(cft[...], x))
            second[slot, pl.ds(at + pairs * pair, pair), :] = stacked(dot(cft[...], y))
        copies.append(pltpu.make_async_copy(second.at[slot], out.at[p], sent.at[slot]))
        copies[-1].start()
    plane = near[0].shape[0]
    for slot in range(plane * len(near)):
        slot_cubes(slot, early, pitch, own, right, dd, near[slot // plane].at[slot % plane])
    for copy in copies:
        copy.wait()


def projections(n, plane, early, slab, cft, dt, vt):
    cols, pixels = slab.shape[0], slab.shape[1]
    rank = dt.shape[0]
    own = rank // n
    anywhere = pl.BlockSpec(memory_space=pl.ANY)
    in_vmem = pl.BlockSpec(memory_space=pltpu.VMEM)
    params = pltpu.CompilerParams(vmem_limit_bytes=56 << 20)
    half = n // plane // 2
    part = [jax.ShapeDtypeStruct((plane, own // 2 * early, pixels), BF16)] * half
    far = pl.pallas_call(
        functools.partial(early_cubes, early, own, n // 2),
        out_shape=[pltpu.VMEM(part[0].shape, BF16)] * half,
        in_specs=[anywhere] * 3,
        out_specs=[in_vmem] * half,
        scratch_shapes=[
            pltpu.VMEM(dt.shape, BF16),
            pltpu.VMEM(vt.shape, BF16),
            pltpu.VMEM((early,) + slab.shape[1:], BF16),
            pltpu.VMEM((rank // 2 * (early + 1), pixels), F32),
            pltpu.SemaphoreType.DMA((2,)),
            pltpu.SemaphoreType.DMA((2,)),
        ],
        compiler_params=params,
    )(slab, dt, vt)
    height = own // 2 * (cols - early) + 2 * own * SCAN_RANK
    *near, second = pl.pallas_call(
        functools.partial(late_cubes, early, own),
        out_shape=part + [jax.ShapeDtypeStruct((n, height, pixels), BF16)],
        in_specs=[in_vmem] * 4,
        out_specs=[in_vmem] * half + [anywhere],
        scratch_shapes=[pltpu.VMEM((rank * (cols + 1), pixels), F32)] * 2
        + [pltpu.VMEM((n, height, pixels), BF16), pltpu.SemaphoreType.DMA((n,))],
        compiler_params=pltpu.CompilerParams(vmem_limit_bytes=32 << 20),
    )(slab, cft, dt, vt)
    return near + list(far), second


def one_hot(shape, rows_per, cols_per):
    r = lax.broadcasted_iota(jnp.int32, shape, 0)
    c = lax.broadcasted_iota(jnp.int32, shape, 1)
    return r // rows_per == c // cols_per


def spread_weights(rft, rows, order=None):
    weights = rft[...]
    if order is not None:
        r = lax.broadcasted_iota(jnp.int32, (rows, rows), 0)
        c = lax.broadcasted_iota(jnp.int32, (rows, rows), 1)
        weights = dot(weights, (r == (c ^ order)).astype(BF16)).astype(BF16)
    tall = one_hot((SCAN_RANK * GROUP, SCAN_RANK), GROUP, 1).astype(BF16)
    wide = one_hot((rows, rows * GROUP), 1, GROUP).astype(BF16)
    weights = dot(dot(tall, weights).astype(BF16), wide)
    r = lax.broadcasted_iota(jnp.int32, weights.shape, 0)
    c = lax.broadcasted_iota(jnp.int32, weights.shape, 1)
    return jnp.where(r % GROUP == c % GROUP, weights, 0.0).astype(BF16)


def wide(get, at, size, pitch, pairs):
    return jnp.concatenate([get(at + h * pitch, size) for h in range(pairs)], axis=1)


def stack_rows(arrays, at, size):
    return jnp.concatenate([x[pl.ds(at, size), :] for x in arrays], axis=0)


def store_unfold(unfold, at, u):
    for i in range(SCAN_RANK):
        unfold[i, pl.ds(at, GROUP), :] = u[i * GROUP : (i + 1) * GROUP]


def early_grams(own, plane, rft, cft, *refs):
    *first, plain, unfold, rowpart, corner = refs
    rows = rft.shape[1]
    pairs = own // 2
    early = first[0].shape[1] // pairs
    me = lax.axis_index("row")
    mixed = spread_weights(rft, rows, me)
    plain[...] = spread_weights(rft, rows)
    slots = [first[s % plane].at[s // plane] for s in range(rows)]
    for c in range(0, early, GROUP):
        x = wide(functools.partial(stack_rows, slots), c, GROUP, early, pairs)
        store_unfold(unfold, c, dot(mixed, x).astype(BF16))
    gram = jnp.zeros((early, early), F32)
    for i in range(SCAN_RANK):
        gram += dot(unfold[i], unfold[i], LAST)
    corner[...] = gram * SCAN_SCALE
    for s in range(rows):
        x = wide(lambda at, size: slots[s][pl.ds(at, size), :], 0, early, early, pairs)
        y = dot(cft[:, :early], x)
        for h in range(pairs):
            rowpart[h, pl.ds(me ^ s, SCAN_RANK, stride=rows), :] = y[:, h * LANES : (h + 1) * LANES]


def partial_grams(own, cft, plain, early_unfold, rowpart, corner, second, keep, send, unfold, rowbuf, total):
    rows, cols, pixels = second.shape[0], cft.shape[1], second.shape[2]
    pairs, half = own // 2, cols // 2
    slots = [second.at[s] for s in range(rows)]
    for c in range(0, half, GROUP):
        x = wide(functools.partial(stack_rows, slots), c, GROUP, half, pairs)
        store_unfold(unfold, c, dot(plain[...], x).astype(BF16))
    side = jnp.zeros((half, half), F32)
    gram = jnp.zeros((half, half), F32)
    for i in range(SCAN_RANK):
        side += dot(early_unfold[i], unfold[i], LAST)
        gram += dot(unfold[i], unfold[i], LAST)
    total[pl.ds(0, half), :] = jnp.concatenate([corner[...], side * SCAN_SCALE], axis=1)
    total[pl.ds(3 * half, half), pl.ds(0, half)] = gram * SCAN_SCALE
    for s in range(rows):
        x = wide(lambda at, size: slots[s][pl.ds(at, size), :], 0, half, half, pairs)
        y = dot(cft[:, half:], x)
        for h in range(pairs):
            rowbuf[h, pl.ds(s, SCAN_RANK, stride=rows), :] = y[:, h * LANES : (h + 1) * LANES]
    gram = jnp.zeros((rows, rows), F32)
    for i in range(SCAN_RANK):
        for h in range(pairs):
            at = pl.ds(i * rows, rows)
            x = (rowbuf[h, at, :] + rowpart[h, at, :]).astype(BF16)
            gram += dot(x, x, LAST)
    spare = jnp.concatenate([gram * SCAN_SCALE, jnp.zeros((rows, half - rows), F32)], axis=1)
    total[pl.ds(5 * half - rows, rows), pl.ds(half, half)] = spare
    n_part = own * SCAN_RANK
    for k in range(2):
        gram = jnp.zeros((pixels, pixels), F32)
        for g in range(n_part // GROUP):
            at = pairs * half + k * n_part + g * GROUP
            u = dot(plain[...], stack_rows(slots, at, GROUP)).astype(BF16)
            gram += dot(u, u, FIRST)
        gram *= DET_SCALE
        total[pl.ds((1 + k) * half, half), :] = gram[:half]
        total[pl.ds((3 + (1 + k) // 2) * half, half), pl.ds((1 + k) % 2 * half, half)] = gram[half:, half:]
    size = keep.shape[0]
    core = lax.axis_index("row") % 2
    keep[...] = total[pl.ds(pl.multiple_of(core * size, 8), size), :]
    send[...] = total[pl.ds(pl.multiple_of((1 - core) * size, 8), size), :]


def unpack(mine, other, row_out, col_out, right_out, left_out, row_gram, grams, sems):
    even = lax.axis_index("row") % 2 == 0
    total = jnp.concatenate(
        [jnp.where(even, mine[...], other[...]), jnp.where(even, other[...], mine[...])], axis=0
    )
    cols, rows = col_out.shape[0], row_out.shape[0]
    half = cols // 2
    copies = []
    for k, out in enumerate([col_out, right_out, left_out]):
        top = total[k * half : (k + 1) * half]
        corner = total[(3 + k // 2) * half : (4 + k // 2) * half, k % 2 * half : (k % 2 + 1) * half]
        grams[k, pl.ds(0, half), :] = top
        grams[k, pl.ds(half, half), :] = jnp.concatenate([top[:, half:].T, corner], axis=1)
        copies.append(pltpu.make_async_copy(grams.at[k], out, sems.at[k]))
        copies[-1].start()
    row_gram[...] = total[5 * half - rows : 5 * half, half : half + rows]
    copies.append(pltpu.make_async_copy(row_gram, row_out, sems.at[3]))
    copies[-1].start()
    for copy in copies:
        copy.wait()


def call(kernel, args, outs, scratch=(), cost=10**8):
    return pl.pallas_call(
        kernel,
        out_shape=[jax.ShapeDtypeStruct(*out) for out in outs],
        scratch_shapes=scratch,
        compiler_params=pltpu.CompilerParams(vmem_limit_bytes=40 << 20),
        cost_estimate=pl.CostEstimate(flops=cost, bytes_accessed=1 << 20, transcendentals=0),
    )(*args)


def swap(x, n, step):
    return lax.ppermute(x, "row", [(i, i ^ step) for i in range(n)])


def by_place(plane, *refs):
    before, after = refs[:-plane], refs[-plane:]
    for z, x in enumerate(before):
        for q, y in enumerate(after):
            y[z] = x[q]


def join_planes(near, *refs):
    plane = (len(refs) - near) // 2
    before, far, after = refs[:near], refs[near : near + plane], refs[near + plane :]
    for q, y in enumerate(after):
        for z, x in enumerate(before):
            y[z] = x[q]
        y[pl.ds(near, y.shape[0] - near)] = far[q][...]


def regrouped(near, far):
    plane, height, width = near[0].shape
    some = [((len(far), height, width), BF16)] * plane
    every = [((len(near) + len(far), height, width), BF16)] * plane
    far = call(functools.partial(by_place, plane), far, some, cost=4 * 10**10)
    return call(functools.partial(join_planes, len(near)), (*near, *far), every)


def all_sum(mine, other, n):
    mine = mine + swap(other, n, 1)
    step = 2
    while step < n:
        mine = mine + swap(mine, n, step)
        step *= 2
    return mine, swap(mine, n, 1)


def local(n, plane, slab, row_factor, col_factor, det_row_factor, det_col_factor):
    slab = slab.reshape(slab.shape[-3:])
    cols, pixels = slab.shape[0], slab.shape[1]
    rows = row_factor.shape[0]
    own = DET_RANK // n
    rft, cft = row_factor.T, col_factor.T
    early = cols // 2
    first, second = projections(n, plane, early, slab, cft, det_row_factor.T, det_col_factor.T)
    first = [x if z == 0 else swap(x, n, z * plane) for z, x in enumerate(first)]
    second = lax.all_to_all(second, "row", split_axis=0, concat_axis=0, tiled=True)
    first = regrouped(first[: plane // 2], first[plane // 2 :])
    first = [x if q == 0 else swap(x, n, q) for q, x in enumerate(first)]
    pairs, width = own // 2, own * DET_RANK
    row_shape = (pairs, SCAN_RANK * rows, LANES)
    shapes = [
        ((SCAN_RANK * GROUP, rows * GROUP), BF16),
        ((SCAN_RANK, early, width), BF16),
        (row_shape, F32),
        ((early, early), F32),
    ]
    known = call(functools.partial(early_grams, own, plane), (rft, cft, *first), shapes)
    scratch = [
        pltpu.VMEM((SCAN_RANK, early, width), BF16),
        pltpu.VMEM(row_shape, F32),
        pltpu.VMEM((5 * cols // 2, pixels), F32),
    ]
    mine, other = call(
        functools.partial(partial_grams, own), (cft, *known, second), [((5 * cols // 4, pixels), F32)] * 2, scratch
    )
    mine, other = all_sum(mine, other, n)
    outs = [(rows, rows), (cols, cols), (pixels, pixels), (pixels, pixels)]
    in_vmem = pl.BlockSpec(memory_space=pltpu.VMEM)
    return pl.pallas_call(
        unpack,
        out_shape=[jax.ShapeDtypeStruct(shape, F32) for shape in outs],
        in_specs=[in_vmem] * 2,
        out_specs=[pl.BlockSpec(memory_space=pl.ANY)] * 4,
        scratch_shapes=[
            pltpu.VMEM((rows, rows), F32),
            pltpu.VMEM((3, cols, cols), F32),
            pltpu.SemaphoreType.DMA((4,)),
        ],
        compiler_params=pltpu.CompilerParams(vmem_limit_bytes=16 << 20),
    )(mine, other)


def plain(n, slab, row_factor, col_factor, det_row_factor, det_col_factor):
    slab = slab.reshape(slab.shape[-3:])
    rows, own = row_factor.shape[0], DET_RANK // n
    half_right = jnp.einsum("ckl,lb->cbk", slab, det_col_factor, preferred_element_type=F32).astype(BF16)
    half_left = jnp.einsum("ckl,ka->cal", slab, det_row_factor, preferred_element_type=F32).astype(BF16)
    cubes = jnp.einsum("cbk,ka->bca", half_right, det_row_factor, preferred_element_type=F32).astype(BF16)
    right_cols = jnp.einsum("cbk,cj->bjk", half_right, col_factor, preferred_element_type=F32).astype(BF16)
    left_cols = jnp.einsum("cal,cj->ajl", half_left, col_factor, preferred_element_type=F32).astype(BF16)
    cubes, right_cols, left_cols = (
        lax.all_to_all(x.reshape((n, own) + x.shape[1:]), "row", split_axis=0, concat_axis=0, tiled=True)
        for x in (cubes, right_cols, left_cols)
    )
    row_unfold = jnp.einsum("rbca,cj->rjba", cubes, col_factor, preferred_element_type=F32).astype(BF16)
    col_unfold = jnp.einsum("rbca,ri->ibca", cubes, row_factor, preferred_element_type=F32).astype(BF16)
    det_right = jnp.einsum("rbjk,ri->ibjk", right_cols, row_factor, preferred_element_type=F32).astype(BF16)
    det_left = jnp.einsum("rajl,ri->iajl", left_cols, row_factor, preferred_element_type=F32).astype(BF16)
    row_gram = jnp.einsum("rjba,sjba->rs", row_unfold, row_unfold, preferred_element_type=F32)
    col_gram = jnp.einsum("ibca,ibda->cd", col_unfold, col_unfold, preferred_element_type=F32)
    right_gram = jnp.einsum("ibjk,ibjm->km", det_right, det_right, preferred_element_type=F32)
    left_gram = jnp.einsum("iajl,iajm->lm", det_left, det_left, preferred_element_type=F32)
    scaled = (row_gram * SCAN_SCALE, col_gram * SCAN_SCALE, right_gram * DET_SCALE, left_gram * DET_SCALE)
    return lax.psum(scaled, "row")


def solution(mesh):
    in_specs = (
        P(("slab", "row"), None, None, None),
        P("slab", None),
        P("slab", None),
        P("slab", None),
        P("slab", None),
    )
    out_specs = (P("slab", None), P("slab", None), P("slab", None), P("slab", None))
    n = mesh.shape["row"]
    plane = round(n**0.5)
    tuned = plane * plane == n and n & (n - 1) == 0 and DET_RANK % (2 * n) == 0
    run = functools.partial(local, n, plane) if tuned else functools.partial(plain, n)
    return jax.shard_map(run, mesh=mesh, in_specs=in_specs, out_specs=out_specs, check_vma=False)
```

```python
import functools

import jax
import jax.numpy as jnp
from jax import lax
from jax.experimental import pallas as pl
from jax.experimental.pallas import tpu as pltpu
from jax.sharding import PartitionSpec as P

DET_RANK = 64
SCAN_RANK = 8
SCAN_SCALE = 1.0 / (SCAN_RANK * DET_RANK * DET_RANK)
DET_SCALE = 1.0 / (SCAN_RANK * SCAN_RANK * DET_RANK)
LANES = 128
GROUP = 16
BF16 = jnp.bfloat16
F32 = jnp.float32
LAST = (((1,), (1,)), ((), ()))
FIRST = (((0,), (0,)), ((), ()))


def dot(x, y, dims=None):
    if dims is None:
        return jnp.dot(x, y, preferred_element_type=F32)
    return lax.dot_general(x, y, dims, preferred_element_type=F32)


def paired(x):
    none = jnp.zeros_like(x)
    return jnp.concatenate([jnp.concatenate([x, none], 1), jnp.concatenate([none, x], 1)], 0)


def four_images(images, c):
    return jnp.concatenate(
        [
            jnp.concatenate([images[c], images[c + 1]], axis=1),
            jnp.concatenate([images[c + 2], images[c + 3]], axis=1),
        ],
        axis=0,
    )


def early_cubes(early, own, base, slab, dt_in, vt_in, *refs):
    *far, dt, vt, images, right, arrived, ready = refs
    pixels = slab.shape[1]
    plane = far[0].shape[0]
    rank = own * plane * len(far)
    pitch = early + 1
    cuts = [0, early // 2, early]
    copies = [
        pltpu.make_async_copy(slab.at[pl.ds(a, b - a)], images.at[pl.ds(a, b - a)], arrived.at[i])
        for i, (a, b) in enumerate(zip(cuts, cuts[1:]))
    ]
    factors = [pltpu.make_async_copy(x, y, ready.at[i]) for i, (x, y) in enumerate([(dt_in, dt), (vt_in, vt)])]
    for copy in factors + copies:
        copy.start()
    for copy in factors:
        copy.wait()
    vt2, dd = paired(slot_order(vt[...], own, base, rank)), paired(dt[...].T)
    for at, copy in enumerate(copies):
        copy.wait()
        for c in range(cuts[at], cuts[at + 1], 4):
            rights = dot(vt2, four_images(images, c), LAST)
            for i in range(2):
                for j in range(2):
                    right[pl.ds(c + 2 * i + j, rank, stride=pitch), :] = rights[
                        j * rank : (j + 1) * rank, i * pixels : (i + 1) * pixels
                    ]
    for slot in range(plane * len(far)):
        slot_cubes(slot, early, pitch, own, right, dd, far[slot // plane].at[slot % plane])


def slot_order(factor, own, base, count):
    shape = (count, factor.shape[0])
    r = lax.broadcasted_iota(jnp.int32, shape, 0) + base * own
    c = lax.broadcasted_iota(jnp.int32, shape, 1)
    take = (c // own == r // own ^ lax.axis_index("row")) & (c % own == r % own)
    return dot(take.astype(BF16), factor).astype(BF16)


def slot_cubes(slot, early, pitch, own, right, dd, to):
    for h in range(own // 2):
        b = slot * own + 2 * h
        x = [right[pl.ds((b + k) * pitch, early), :] for k in range(2)]
        to[pl.ds(h * early, early), :] = dot(jnp.concatenate(x, axis=1).astype(BF16), dd).astype(BF16)


def late_cubes(early, own, images, cft, dt, vt, *refs):
    *near, out, right, left, second, sent = refs
    cols, pixels, rank = images.shape[0], images.shape[1], dt.shape[0]
    pitch = cols + 1
    dt2, vt2 = (paired(slot_order(x[...], own, 0, rank)) for x in (dt, vt))
    for c in range(0, cols, 4):
        four = four_images(images, c)
        rights = dot(vt2, four, LAST)
        lefts = dot(dt2, four)
        for i in range(2):
            for j in range(2):
                at_c = pl.ds(c + 2 * i + j, rank, stride=pitch)
                right[at_c, :] = rights[j * rank : (j + 1) * rank, i * pixels : (i + 1) * pixels]
                left[at_c, :] = lefts[i * rank : (i + 1) * rank, j * pixels : (j + 1) * pixels]
    dd = paired(dt[...].T)
    pairs, pair = own // 2, 2 * SCAN_RANK
    late = cols - early

    def two(ref, b):
        parts = [ref[pl.ds((b + k) * pitch, cols), :] for k in range(2)]
        return jnp.concatenate(parts, axis=1).astype(BF16)

    def stacked(sums):
        return jnp.concatenate([sums[:, :pixels], sums[:, pixels:]], axis=0).astype(BF16)

    me = lax.axis_index("row")
    copies = []
    for slot in range(rank // own):
        p = me ^ slot
        for h in range(pairs):
            x = two(right, slot * own + 2 * h)
            y = two(left, slot * own + 2 * h)
            at = pairs * late + h * pair
            second[slot, pl.ds(h * late, late), :] = dot(x[early:], dd).astype(BF16)
            second[slot, pl.ds(at, pair), :] = stacked(dot(cft[...], x))
            second[slot, pl.ds(at + pairs * pair, pair), :] = stacked(dot(cft[...], y))
        copies.append(pltpu.make_async_copy(second.at[slot], out.at[p], sent.at[slot]))
        copies[-1].start()
    plane = near[0].shape[0]
    for slot in range(plane * len(near)):
        slot_cubes(slot, early, pitch, own, right, dd, near[slot // plane].at[slot % plane])
    for copy in copies:
        copy.wait()


def projections(n, plane, early, slab, cft, dt, vt):
    cols, pixels = slab.shape[0], slab.shape[1]
    rank = dt.shape[0]
    own = rank // n
    anywhere = pl.BlockSpec(memory_space=pl.ANY)
    in_vmem = pl.BlockSpec(memory_space=pltpu.VMEM)
    params = pltpu.CompilerParams(vmem_limit_bytes=56 << 20)
    half = n // plane // 2
    part = [jax.ShapeDtypeStruct((plane, own // 2 * early, pixels), BF16)] * half
    far = pl.pallas_call(
        functools.partial(early_cubes, early, own, n // 2),
        out_shape=[pltpu.VMEM(part[0].shape, BF16)] * half,
        in_specs=[anywhere] * 3,
        out_specs=[in_vmem] * half,
        scratch_shapes=[
            pltpu.VMEM(dt.shape, BF16),
            pltpu.VMEM(vt.shape, BF16),
            pltpu.VMEM((early,) + slab.shape[1:], BF16),
            pltpu.VMEM((rank // 2 * (early + 1), pixels), F32),
            pltpu.SemaphoreType.DMA((2,)),
            pltpu.SemaphoreType.DMA((2,)),
        ],
        compiler_params=params,
    )(slab, dt, vt)
    height = own // 2 * (cols - early) + 2 * own * SCAN_RANK
    *near, second = pl.pallas_call(
        functools.partial(late_cubes, early, own),
        out_shape=part + [jax.ShapeDtypeStruct((n, height, pixels), BF16)],
        in_specs=[in_vmem] * 4,
        out_specs=[in_vmem] * half + [anywhere],
        scratch_shapes=[pltpu.VMEM((rank * (cols + 1), pixels), F32)] * 2
        + [pltpu.VMEM((n, height, pixels), BF16), pltpu.SemaphoreType.DMA((n,))],
        compiler_params=pltpu.CompilerParams(vmem_limit_bytes=32 << 20),
    )(slab, cft, dt, vt)
    return near + list(far), second


def one_hot(shape, rows_per, cols_per):
    r = lax.broadcasted_iota(jnp.int32, shape, 0)
    c = lax.broadcasted_iota(jnp.int32, shape, 1)
    return r // rows_per == c // cols_per


def spread_weights(rft, rows, order=None):
    weights = rft[...]
    if order is not None:
        r = lax.broadcasted_iota(jnp.int32, (rows, rows), 0)
        c = lax.broadcasted_iota(jnp.int32, (rows, rows), 1)
        weights = dot(weights, (r == (c ^ order)).astype(BF16)).astype(BF16)
    tall = one_hot((SCAN_RANK * GROUP, SCAN_RANK), GROUP, 1).astype(BF16)
    wide = one_hot((rows, rows * GROUP), 1, GROUP).astype(BF16)
    weights = dot(dot(tall, weights).astype(BF16), wide)
    r = lax.broadcasted_iota(jnp.int32, weights.shape, 0)
    c = lax.broadcasted_iota(jnp.int32, weights.shape, 1)
    return jnp.where(r % GROUP == c % GROUP, weights, 0.0).astype(BF16)


def wide(get, at, size, pitch, pairs):
    return jnp.concatenate([get(at + h * pitch, size) for h in range(pairs)], axis=1)


def stack_rows(arrays, at, size):
    return jnp.concatenate([x[pl.ds(at, size), :] for x in arrays], axis=0)


def store_unfold(unfold, at, u):
    for i in range(SCAN_RANK):
        unfold[i, pl.ds(at, GROUP), :] = u[i * GROUP : (i + 1) * GROUP]


def early_grams(own, plane, rft, cft, *refs):
    *first, plain, unfold, rowpart, corner = refs
    rows = rft.shape[1]
    pairs = own // 2
    early = first[0].shape[1] // pairs
    me = lax.axis_index("row")
    mixed = spread_weights(rft, rows, me)
    plain[...] = spread_weights(rft, rows)
    slots = [first[s % plane].at[s // plane] for s in range(rows)]
    for c in range(0, early, GROUP):
        x = wide(functools.partial(stack_rows, slots), c, GROUP, early, pairs)
        store_unfold(unfold, c, dot(mixed, x).astype(BF16))
    gram = jnp.zeros((early, early), F32)
    for i in range(SCAN_RANK):
        gram += dot(unfold[i], unfold[i], LAST)
    corner[...] = gram * SCAN_SCALE
    for s in range(rows):
        x = wide(lambda at, size: slots[s][pl.ds(at, size), :], 0, early, early, pairs)
        y = dot(cft[:, :early], x)
        for h in range(pairs):
            rowpart[h, pl.ds(me ^ s, SCAN_RANK, stride=rows), :] = y[:, h * LANES : (h + 1) * LANES]


def partial_grams(own, cft, plain, early_unfold, rowpart, corner, second, keep, send, unfold, rowbuf, total):
    rows, cols, pixels = second.shape[0], cft.shape[1], second.shape[2]
    pairs, half = own // 2, cols // 2
    slots = [second.at[s] for s in range(rows)]
    for c in range(0, half, GROUP):
        x = wide(functools.partial(stack_rows, slots), c, GROUP, half, pairs)
        store_unfold(unfold, c, dot(plain[...], x).astype(BF16))
    side = jnp.zeros((half, half), F32)
    gram = jnp.zeros((half, half), F32)
    for i in range(SCAN_RANK):
        side += dot(early_unfold[i], unfold[i], LAST)
        gram += dot(unfold[i], unfold[i], LAST)
    pack(total, 0, jnp.concatenate([corner[...], side * SCAN_SCALE], axis=1), gram * SCAN_SCALE)
    for s in range(rows):
        x = wide(lambda at, size: slots[s][pl.ds(at, size), :], 0, half, half, pairs)
        y = dot(cft[:, half:], x)
        for h in range(pairs):
            rowbuf[h, pl.ds(s, SCAN_RANK, stride=rows), :] = y[:, h * LANES : (h + 1) * LANES]
    gram = jnp.zeros((rows, rows), F32)
    for i in range(SCAN_RANK):
        for h in range(pairs):
            at = pl.ds(i * rows, rows)
            x = (rowbuf[h, at, :] + rowpart[h, at, :]).astype(BF16)
            gram += dot(x, x, LAST)
    spare = jnp.concatenate([gram * SCAN_SCALE, jnp.zeros((rows, half - rows), F32)], axis=1)
    total[pl.ds(4 * half - rows, rows), pl.ds(half, half)] = spare
    n_part = own * SCAN_RANK
    for k in range(2):
        gram = jnp.zeros((pixels, pixels), F32)
        for g in range(n_part // GROUP):
            at = pairs * half + k * n_part + g * GROUP
            u = dot(plain[...], stack_rows(slots, at, GROUP)).astype(BF16)
            gram += dot(u, u, FIRST)
        gram *= DET_SCALE
        pack(total, 1 + k, gram[:half], gram[half:, half:])
    size = keep.shape[0]
    core = lax.axis_index("row") % 2
    keep[...] = total[pl.ds(pl.multiple_of(core * size, 8), size), :]
    send[...] = total[pl.ds(pl.multiple_of((1 - core) * size, 8), size), :]


def pack(total, k, top, low):
    half, part = low.shape[0], low.shape[0] // 2
    total[pl.ds(k * half, part), :] = top[:part]
    total[pl.ds(k * half + part, part), :] = jnp.concatenate([low[part:, part:], top[part:, part:]], axis=1)
    total[pl.ds(3 * half + k // 2 * part, part), pl.ds(k % 2 * half, half)] = low[:part]


def unpack(mine, other, row_out, col_out, right_out, left_out, row_gram, grams, sems):
    even = lax.axis_index("row") % 2 == 0
    total = jnp.concatenate(
        [jnp.where(even, mine[...], other[...]), jnp.where(even, other[...], mine[...])], axis=0
    )
    cols, rows = col_out.shape[0], row_out.shape[0]
    half, part = cols // 2, cols // 4
    copies = []
    for k, out in enumerate([col_out, right_out, left_out]):
        top = total[k * half : k * half + part]
        next_top = total[k * half + part : (k + 1) * half]
        low = total[3 * half + k // 2 * part :][:part, k % 2 * half : (k % 2 + 1) * half]
        side = jnp.concatenate([top[:, half:], next_top[:, half:]], axis=0).T
        last = [side[part:], low[:, part:].T, next_top[:, :part]]
        grams[k, pl.ds(0, part), :] = top
        grams[k, pl.ds(part, part), :] = jnp.concatenate([top[:, part:half].T, next_top[:, part:]], axis=1)
        grams[k, pl.ds(half, part), :] = jnp.concatenate([side[:part], low], axis=1)
        grams[k, pl.ds(half + part, part), :] = jnp.concatenate(last, axis=1)
        copies.append(pltpu.make_async_copy(grams.at[k], out, sems.at[k]))
        copies[-1].start()
    row_gram[...] = total[4 * half - rows : 4 * half, half : half + rows]
    copies.append(pltpu.make_async_copy(row_gram, row_out, sems.at[3]))
    copies[-1].start()
    for copy in copies:
        copy.wait()


def call(kernel, args, outs, scratch=(), cost=10**8):
    return pl.pallas_call(
        kernel,
        out_shape=[jax.ShapeDtypeStruct(*out) for out in outs],
        scratch_shapes=scratch,
        compiler_params=pltpu.CompilerParams(vmem_limit_bytes=40 << 20),
        cost_estimate=pl.CostEstimate(flops=cost, bytes_accessed=1 << 20, transcendentals=0),
    )(*args)


def swap(x, n, step):
    return lax.ppermute(x, "row", [(i, i ^ step) for i in range(n)])


def by_place(plane, *refs):
    before, after = refs[:-plane], refs[-plane:]
    for z, x in enumerate(before):
        for q, y in enumerate(after):
            y[z] = x[q]


def join_planes(near, *refs):
    plane = (len(refs) - near) // 2
    before, far, after = refs[:near], refs[near : near + plane], refs[near + plane :]
    for q, y in enumerate(after):
        for z, x in enumerate(before):
            y[z] = x[q]
        y[pl.ds(near, y.shape[0] - near)] = far[q][...]


def regrouped(near, far):
    plane, height, width = near[0].shape
    some = [((len(far), height, width), BF16)] * plane
    every = [((len(near) + len(far), height, width), BF16)] * plane
    far = call(functools.partial(by_place, plane), far, some, cost=4 * 10**10)
    return call(functools.partial(join_planes, len(near)), (*near, *far), every)


def all_sum(mine, other, n):
    mine = mine + swap(other, n, 1)
    step = 2
    while step < n:
        mine = mine + swap(mine, n, step)
        step *= 2
    return mine, swap(mine, n, 1)


def local(n, plane, slab, row_factor, col_factor, det_row_factor, det_col_factor):
    slab = slab.reshape(slab.shape[-3:])
    cols, pixels = slab.shape[0], slab.shape[1]
    rows = row_factor.shape[0]
    own = DET_RANK // n
    rft, cft = row_factor.T, col_factor.T
    early = cols // 2
    first, second = projections(n, plane, early, slab, cft, det_row_factor.T, det_col_factor.T)
    first = [x if z == 0 else swap(x, n, z * plane) for z, x in enumerate(first)]
    second = lax.all_to_all(second, "row", split_axis=0, concat_axis=0, tiled=True)
    first = regrouped(first[: plane // 2], first[plane // 2 :])
    first = [x if q == 0 else swap(x, n, q) for q, x in enumerate(first)]
    pairs, width = own // 2, own * DET_RANK
    row_shape = (pairs, SCAN_RANK * rows, LANES)
    shapes = [
        ((SCAN_RANK * GROUP, rows * GROUP), BF16),
        ((SCAN_RANK, early, width), BF16),
        (row_shape, F32),
        ((early, early), F32),
    ]
    known = call(functools.partial(early_grams, own, plane), (rft, cft, *first), shapes)
    scratch = [
        pltpu.VMEM((SCAN_RANK, early, width), BF16),
        pltpu.VMEM(row_shape, F32),
        pltpu.VMEM((2 * cols, pixels), F32),
    ]
    mine, other = call(
        functools.partial(partial_grams, own), (cft, *known, second), [((cols, pixels), F32)] * 2, scratch
    )
    mine, other = all_sum(mine, other, n)
    outs = [(rows, rows), (cols, cols), (pixels, pixels), (pixels, pixels)]
    in_vmem = pl.BlockSpec(memory_space=pltpu.VMEM)
    return pl.pallas_call(
        unpack,
        out_shape=[jax.ShapeDtypeStruct(shape, F32) for shape in outs],
        in_specs=[in_vmem] * 2,
        out_specs=[pl.BlockSpec(memory_space=pl.ANY)] * 4,
        scratch_shapes=[
            pltpu.VMEM((rows, rows), F32),
            pltpu.VMEM((3, cols, cols), F32),
            pltpu.SemaphoreType.DMA((4,)),
        ],
        compiler_params=pltpu.CompilerParams(vmem_limit_bytes=16 << 20),
    )(mine, other)


def plain(n, slab, row_factor, col_factor, det_row_factor, det_col_factor):
    slab = slab.reshape(slab.shape[-3:])
    rows, own = row_factor.shape[0], DET_RANK // n
    half_right = jnp.einsum("ckl,lb->cbk", slab, det_col_factor, preferred_element_type=F32).astype(BF16)
    half_left = jnp.einsum("ckl,ka->cal", slab, det_row_factor, preferred_element_type=F32).astype(BF16)
    cubes = jnp.einsum("cbk,ka->bca", half_right, det_row_factor, preferred_element_type=F32).astype(BF16)
    right_cols = jnp.einsum("cbk,cj->bjk", half_right, col_factor, preferred_element_type=F32).astype(BF16)
    left_cols = jnp.einsum("cal,cj->ajl", half_left, col_factor, preferred_element_type=F32).astype(BF16)
    cubes, right_cols, left_cols = (
        lax.all_to_all(x.reshape((n, own) + x.shape[1:]), "row", split_axis=0, concat_axis=0, tiled=True)
        for x in (cubes, right_cols, left_cols)
    )
    row_unfold = jnp.einsum("rbca,cj->rjba", cubes, col_factor, preferred_element_type=F32).astype(BF16)
    col_unfold = jnp.einsum("rbca,ri->ibca", cubes, row_factor, preferred_element_type=F32).astype(BF16)
    det_right = jnp.einsum("rbjk,ri->ibjk", right_cols, row_factor, preferred_element_type=F32).astype(BF16)
    det_left = jnp.einsum("rajl,ri->iajl", left_cols, row_factor, preferred_element_type=F32).astype(BF16)
    row_gram = jnp.einsum("rjba,sjba->rs", row_unfold, row_unfold, preferred_element_type=F32)
    col_gram = jnp.einsum("ibca,ibda->cd", col_unfold, col_unfold, preferred_element_type=F32)
    right_gram = jnp.einsum("ibjk,ibjm->km", det_right, det_right, preferred_element_type=F32)
    left_gram = jnp.einsum("iajl,iajm->lm", det_left, det_left, preferred_element_type=F32)
    scaled = (row_gram * SCAN_SCALE, col_gram * SCAN_SCALE, right_gram * DET_SCALE, left_gram * DET_SCALE)
    return lax.psum(scaled, "row")


def solution(mesh):
    in_specs = (
        P(("slab", "row"), None, None, None),
        P("slab", None),
        P("slab", None),
        P("slab", None),
        P("slab", None),
    )
    out_specs = (P("slab", None), P("slab", None), P("slab", None), P("slab", None))
    n = mesh.shape["row"]
    plane = round(n**0.5)
    tuned = plane * plane == n and n & (n - 1) == 0 and DET_RANK % (2 * n) == 0
    run = functools.partial(local, n, plane) if tuned else functools.partial(plain, n)
    return jax.shard_map(run, mesh=mesh, in_specs=in_specs, out_specs=out_specs, check_vma=False)
```

```python
import functools

import jax
import jax.numpy as jnp
from jax import lax
from jax.experimental import pallas as pl
from jax.experimental.pallas import tpu as pltpu
from jax.sharding import PartitionSpec as P

DET_RANK = 64
SCAN_RANK = 8
SCAN_SCALE = 1.0 / (SCAN_RANK * DET_RANK * DET_RANK)
DET_SCALE = 1.0 / (SCAN_RANK * SCAN_RANK * DET_RANK)
LANES = 128
GROUP = 16
BF16 = jnp.bfloat16
F32 = jnp.float32
LAST = (((1,), (1,)), ((), ()))
FIRST = (((0,), (0,)), ((), ()))


def dot(x, y, dims=None):
    if dims is None:
        return jnp.dot(x, y, preferred_element_type=F32)
    return lax.dot_general(x, y, dims, preferred_element_type=F32)


def paired(x):
    none = jnp.zeros_like(x)
    return jnp.concatenate([jnp.concatenate([x, none], 1), jnp.concatenate([none, x], 1)], 0)


def four_images(images, c):
    return jnp.concatenate(
        [
            jnp.concatenate([images[c], images[c + 1]], axis=1),
            jnp.concatenate([images[c + 2], images[c + 3]], axis=1),
        ],
        axis=0,
    )


def early_cubes(early, own, slab, dt_in, vt_in, *refs):
    *first, kept, dt, vt, images, right, arrived, ready = refs
    pixels = slab.shape[1]
    plane, rank = first[0].shape[0], dt.shape[0]
    pitch = early + 1
    cuts = [0, early // 2, early]
    copies = [
        pltpu.make_async_copy(slab.at[pl.ds(a, b - a)], images.at[pl.ds(a, b - a)], arrived.at[i])
        for i, (a, b) in enumerate(zip(cuts, cuts[1:]))
    ]
    factors = [pltpu.make_async_copy(x, y, ready.at[i]) for i, (x, y) in enumerate([(dt_in, dt), (vt_in, vt)])]
    for copy in factors + copies:
        copy.start()
    for copy in factors:
        copy.wait()
    vt2, dd = paired(slot_order(vt[...], own)), paired(dt[...].T)
    for at, copy in enumerate(copies):
        copy.wait()
        for c in range(cuts[at], cuts[at + 1], 4):
            rights = dot(vt2, four_images(images, c), LAST)
            for i in range(2):
                for j in range(2):
                    right[pl.ds(c + 2 * i + j, rank, stride=pitch), :] = rights[
                        j * rank : (j + 1) * rank, i * pixels : (i + 1) * pixels
                    ]
    for slot in range(rank // own):
        to = first[slot // plane].at[slot % plane]
        for h in range(own // 2):
            b = slot * own + 2 * h
            x = [right[pl.ds((b + k) * pitch, early), :] for k in range(2)]
            x = jnp.concatenate(x, axis=1).astype(BF16)
            kept[b // 2] = x
            to[pl.ds(h * early, early), :] = dot(x, dd).astype(BF16)


def slot_order(factor, own):
    shape = (factor.shape[0], factor.shape[0])
    r = lax.broadcasted_iota(jnp.int32, shape, 0)
    c = lax.broadcasted_iota(jnp.int32, shape, 1)
    take = (c // own == r // own ^ lax.axis_index("row")) & (c % own == r % own)
    return dot(take.astype(BF16), factor).astype(BF16)


def late_cubes(own, images, cft, dt, vt, kept, out, right, left, second, sent):
    cols, pixels, rank = images.shape[0], images.shape[1], dt.shape[0]
    early = kept.shape[1]
    late = cols - early
    dt2, vt2 = (paired(slot_order(x[...], own)) for x in (dt, vt))
    for c in range(0, cols, 4):
        four = four_images(images, c)
        lefts = dot(dt2, four)
        if c >= early:
            rights = dot(vt2, four, LAST)
        for i in range(2):
            for j in range(2):
                at = c + 2 * i + j
                left[pl.ds(at, rank, stride=cols + 1), :] = lefts[
                    i * rank : (i + 1) * rank, j * pixels : (j + 1) * pixels
                ]
                if c >= early:
                    right[pl.ds(at - early, rank, stride=late + 1), :] = rights[
                        j * rank : (j + 1) * rank, i * pixels : (i + 1) * pixels
                    ]
    dd = paired(dt[...].T)
    pairs, pair = own // 2, 2 * SCAN_RANK

    def two(ref, b, count):
        parts = [ref[pl.ds((b + k) * (count + 1), count), :] for k in range(2)]
        return jnp.concatenate(parts, axis=1).astype(BF16)

    def stacked(sums):
        return jnp.concatenate([sums[:, :pixels], sums[:, pixels:]], axis=0).astype(BF16)

    me = lax.axis_index("row")
    copies = []
    for slot in range(rank // own):
        for h in range(pairs):
            b = slot * own + 2 * h
            x = two(right, b, late)
            y = two(left, b, cols)
            at = pairs * late + h * pair
            second[slot, pl.ds(h * late, late), :] = dot(x, dd).astype(BF16)
            x = jnp.concatenate([kept[b // 2], x], axis=0)
            second[slot, pl.ds(at, pair), :] = stacked(dot(cft[...], x))
            second[slot, pl.ds(at + pairs * pair, pair), :] = stacked(dot(cft[...], y))
        copies.append(pltpu.make_async_copy(second.at[slot], out.at[me ^ slot], sent.at[slot]))
        copies[-1].start()
    for copy in copies:
        copy.wait()


def projections(n, plane, early, slab, cft, dt, vt):
    cols, pixels = slab.shape[0], slab.shape[1]
    rank = dt.shape[0]
    own = rank // n
    anywhere = pl.BlockSpec(memory_space=pl.ANY)
    in_vmem = pl.BlockSpec(memory_space=pltpu.VMEM)
    params = pltpu.CompilerParams(vmem_limit_bytes=56 << 20)
    *first, kept = pl.pallas_call(
        functools.partial(early_cubes, early, own),
        out_shape=[pltpu.VMEM((plane, own // 2 * early, pixels), BF16)] * (n // plane)
        + [pltpu.VMEM((rank // 2, early, 2 * pixels), BF16)],
        in_specs=[anywhere] * 3,
        out_specs=[in_vmem] * (n // plane + 1),
        scratch_shapes=[
            pltpu.VMEM(dt.shape, BF16),
            pltpu.VMEM(vt.shape, BF16),
            pltpu.VMEM((early,) + slab.shape[1:], BF16),
            pltpu.VMEM((rank * (early + 1), pixels), F32),
            pltpu.SemaphoreType.DMA((2,)),
            pltpu.SemaphoreType.DMA((2,)),
        ],
        compiler_params=params,
    )(slab, dt, vt)
    late = cols - early
    height = own // 2 * late + 2 * own * SCAN_RANK
    second = pl.pallas_call(
        functools.partial(late_cubes, own),
        out_shape=jax.ShapeDtypeStruct((n, height, pixels), BF16),
        in_specs=[in_vmem] * 5,
        out_specs=anywhere,
        scratch_shapes=[
            pltpu.VMEM((rank * (late + 1), pixels), F32),
            pltpu.VMEM((rank * (cols + 1), pixels), F32),
            pltpu.VMEM((n, height, pixels), BF16),
            pltpu.SemaphoreType.DMA((n,)),
        ],
        compiler_params=pltpu.CompilerParams(vmem_limit_bytes=32 << 20),
    )(slab, cft, dt, vt, kept)
    return first, second


def one_hot(shape, rows_per, cols_per):
    r = lax.broadcasted_iota(jnp.int32, shape, 0)
    c = lax.broadcasted_iota(jnp.int32, shape, 1)
    return r // rows_per == c // cols_per


def spread_weights(rft, rows, order=None):
    weights = rft[...]
    if order is not None:
        r = lax.broadcasted_iota(jnp.int32, (rows, rows), 0)
        c = lax.broadcasted_iota(jnp.int32, (rows, rows), 1)
        weights = dot(weights, (r == (c ^ order)).astype(BF16)).astype(BF16)
    tall = one_hot((SCAN_RANK * GROUP, SCAN_RANK), GROUP, 1).astype(BF16)
    wide = one_hot((rows, rows * GROUP), 1, GROUP).astype(BF16)
    weights = dot(dot(tall, weights).astype(BF16), wide)
    r = lax.broadcasted_iota(jnp.int32, weights.shape, 0)
    c = lax.broadcasted_iota(jnp.int32, weights.shape, 1)
    return jnp.where(r % GROUP == c % GROUP, weights, 0.0).astype(BF16)


def wide(get, at, size, pitch, pairs):
    return jnp.concatenate([get(at + h * pitch, size) for h in range(pairs)], axis=1)


def stack_rows(arrays, at, size):
    return jnp.concatenate([x[pl.ds(at, size), :] for x in arrays], axis=0)


def store_unfold(unfold, at, u):
    for i in range(SCAN_RANK):
        unfold[i, pl.ds(at, GROUP), :] = u[i * GROUP : (i + 1) * GROUP]


def early_grams(own, plane, rft, cft, *refs):
    *first, plain, unfold, rowpart, corner = refs
    rows = rft.shape[1]
    pairs = own // 2
    early = first[0].shape[1] // pairs
    me = lax.axis_index("row")
    mixed = spread_weights(rft, rows, me)
    plain[...] = spread_weights(rft, rows)
    slots = [first[s % plane].at[s // plane] for s in range(rows)]
    for c in range(0, early, GROUP):
        x = wide(functools.partial(stack_rows, slots), c, GROUP, early, pairs)
        store_unfold(unfold, c, dot(mixed, x).astype(BF16))
    gram = jnp.zeros((early, early), F32)
    for i in range(SCAN_RANK):
        gram += dot(unfold[i], unfold[i], LAST)
    corner[...] = gram * SCAN_SCALE
    for s in range(rows):
        x = wide(lambda at, size: slots[s][pl.ds(at, size), :], 0, early, early, pairs)
        y = dot(cft[:, :early], x)
        for h in range(pairs):
            rowpart[h, pl.ds(me ^ s, SCAN_RANK, stride=rows), :] = y[:, h * LANES : (h + 1) * LANES]


def partial_grams(own, cft, plain, early_unfold, rowpart, corner, second, keep, send, unfold, rowbuf, total):
    rows, cols, pixels = second.shape[0], cft.shape[1], second.shape[2]
    pairs, half = own // 2, cols // 2
    slots = [second.at[s] for s in range(rows)]
    for c in range(0, half, GROUP):
        x = wide(functools.partial(stack_rows, slots), c, GROUP, half, pairs)
        store_unfold(unfold, c, dot(plain[...], x).astype(BF16))
    side = jnp.zeros((half, half), F32)
    gram = jnp.zeros((half, half), F32)
    for i in range(SCAN_RANK):
        side += dot(early_unfold[i], unfold[i], LAST)
        gram += dot(unfold[i], unfold[i], LAST)
    pack(total, 0, jnp.concatenate([corner[...], side * SCAN_SCALE], axis=1), gram * SCAN_SCALE)
    for s in range(rows):
        x = wide(lambda at, size: slots[s][pl.ds(at, size), :], 0, half, half, pairs)
        y = dot(cft[:, half:], x)
        for h in range(pairs):
            rowbuf[h, pl.ds(s, SCAN_RANK, stride=rows), :] = y[:, h * LANES : (h + 1) * LANES]
    gram = jnp.zeros((rows, rows), F32)
    for i in range(SCAN_RANK):
        for h in range(pairs):
            at = pl.ds(i * rows, rows)
            x = (rowbuf[h, at, :] + rowpart[h, at, :]).astype(BF16)
            gram += dot(x, x, LAST)
    spare = jnp.concatenate([gram * SCAN_SCALE, jnp.zeros((rows, half - rows), F32)], axis=1)
    total[pl.ds(4 * half - rows, rows), pl.ds(half, half)] = spare
    n_part = own * SCAN_RANK
    for k in range(2):
        gram = jnp.zeros((pixels, pixels), F32)
        for g in range(n_part // GROUP):
            at = pairs * half + k * n_part + g * GROUP
            u = dot(plain[...], stack_rows(slots, at, GROUP)).astype(BF16)
            gram += dot(u, u, FIRST)
        gram *= DET_SCALE
        pack(total, 1 + k, gram[:half], gram[half:, half:])
    size = keep.shape[0]
    core = lax.axis_index("row") % 2
    keep[...] = total[pl.ds(pl.multiple_of(core * size, 8), size), :]
    send[...] = total[pl.ds(pl.multiple_of((1 - core) * size, 8), size), :]


def pack(total, k, top, low):
    half, part = low.shape[0], low.shape[0] // 2
    total[pl.ds(k * half, part), :] = top[:part]
    total[pl.ds(k * half + part, part), :] = jnp.concatenate([low[part:, part:], top[part:, part:]], axis=1)
    total[pl.ds(3 * half + k // 2 * part, part), pl.ds(k % 2 * half, half)] = low[:part]


def unpack(mine, other, row_out, col_out, right_out, left_out, row_gram, grams, sems):
    even = lax.axis_index("row") % 2 == 0
    total = jnp.concatenate(
        [jnp.where(even, mine[...], other[...]), jnp.where(even, other[...], mine[...])], axis=0
    )
    cols, rows = col_out.shape[0], row_out.shape[0]
    half, part = cols // 2, cols // 4
    copies = []
    for k, out in enumerate([col_out, right_out, left_out]):
        top = total[k * half : k * half + part]
        next_top = total[k * half + part : (k + 1) * half]
        low = total[3 * half + k // 2 * part :][:part, k % 2 * half : (k % 2 + 1) * half]
        side = jnp.concatenate([top[:, half:], next_top[:, half:]], axis=0).T
        last = [side[part:], low[:, part:].T, next_top[:, :part]]
        grams[k, pl.ds(0, part), :] = top
        grams[k, pl.ds(part, part), :] = jnp.concatenate([top[:, part:half].T, next_top[:, part:]], axis=1)
        grams[k, pl.ds(half, part), :] = jnp.concatenate([side[:part], low], axis=1)
        grams[k, pl.ds(half + part, part), :] = jnp.concatenate(last, axis=1)
        copies.append(pltpu.make_async_copy(grams.at[k], out, sems.at[k]))
        copies[-1].start()
    row_gram[...] = total[4 * half - rows : 4 * half, half : half + rows]
    copies.append(pltpu.make_async_copy(row_gram, row_out, sems.at[3]))
    copies[-1].start()
    for copy in copies:
        copy.wait()


def call(kernel, args, outs, scratch=(), cost=10**8):
    return pl.pallas_call(
        kernel,
        out_shape=[jax.ShapeDtypeStruct(*out) for out in outs],
        scratch_shapes=scratch,
        compiler_params=pltpu.CompilerParams(vmem_limit_bytes=40 << 20),
        cost_estimate=pl.CostEstimate(flops=cost, bytes_accessed=1 << 20, transcendentals=0),
    )(*args)


def swap(x, n, step):
    return lax.ppermute(x, "row", [(i, i ^ step) for i in range(n)])


def by_place(plane, *refs):
    before, after = refs[:-plane], refs[-plane:]
    for z, x in enumerate(before):
        for q, y in enumerate(after):
            y[z] = x[q]


def join_planes(near, *refs):
    plane = (len(refs) - near) // 2
    before, far, after = refs[:near], refs[near : near + plane], refs[near + plane :]
    for q, y in enumerate(after):
        for z, x in enumerate(before):
            y[z] = x[q]
        y[pl.ds(near, y.shape[0] - near)] = far[q][...]


def regrouped(near, far):
    plane, height, width = near[0].shape
    some = [((len(far), height, width), BF16)] * plane
    every = [((len(near) + len(far), height, width), BF16)] * plane
    far = call(functools.partial(by_place, plane), far, some, cost=4 * 10**10)
    return call(functools.partial(join_planes, len(near)), (*near, *far), every)


def all_sum(mine, other, n):
    mine = mine + swap(other, n, 1)
    step = 2
    while step < n:
        mine = mine + swap(mine, n, step)
        step *= 2
    return mine, swap(mine, n, 1)


def local(n, plane, slab, row_factor, col_factor, det_row_factor, det_col_factor):
    slab = slab.reshape(slab.shape[-3:])
    cols, pixels = slab.shape[0], slab.shape[1]
    rows = row_factor.shape[0]
    own = DET_RANK // n
    rft, cft = row_factor.T, col_factor.T
    early = cols // 2
    first, second = projections(n, plane, early, slab, cft, det_row_factor.T, det_col_factor.T)
    first = [x if z == 0 else swap(x, n, z * plane) for z, x in enumerate(first)]
    second = lax.all_to_all(second, "row", split_axis=0, concat_axis=0, tiled=True)
    first = regrouped(first[: plane // 2], first[plane // 2 :])
    first = [x if q == 0 else swap(x, n, q) for q, x in enumerate(first)]
    pairs, width = own // 2, own * DET_RANK
    row_shape = (pairs, SCAN_RANK * rows, LANES)
    shapes = [
        ((SCAN_RANK * GROUP, rows * GROUP), BF16),
        ((SCAN_RANK, early, width), BF16),
        (row_shape, F32),
        ((early, early), F32),
    ]
    known = call(functools.partial(early_grams, own, plane), (rft, cft, *first), shapes)
    scratch = [
        pltpu.VMEM((SCAN_RANK, early, width), BF16),
        pltpu.VMEM(row_shape, F32),
        pltpu.VMEM((2 * cols, pixels), F32),
    ]
    mine, other = call(
        functools.partial(partial_grams, own), (cft, *known, second), [((cols, pixels), F32)] * 2, scratch
    )
    mine, other = all_sum(mine, other, n)
    outs = [(rows, rows), (cols, cols), (pixels, pixels), (pixels, pixels)]
    in_vmem = pl.BlockSpec(memory_space=pltpu.VMEM)
    return pl.pallas_call(
        unpack,
        out_shape=[jax.ShapeDtypeStruct(shape, F32) for shape in outs],
        in_specs=[in_vmem] * 2,
        out_specs=[pl.BlockSpec(memory_space=pl.ANY)] * 4,
        scratch_shapes=[
            pltpu.VMEM((rows, rows), F32),
            pltpu.VMEM((3, cols, cols), F32),
            pltpu.SemaphoreType.DMA((4,)),
        ],
        compiler_params=pltpu.CompilerParams(vmem_limit_bytes=16 << 20),
    )(mine, other)


def plain(n, slab, row_factor, col_factor, det_row_factor, det_col_factor):
    slab = slab.reshape(slab.shape[-3:])
    rows, own = row_factor.shape[0], DET_RANK // n
    half_right = jnp.einsum("ckl,lb->cbk", slab, det_col_factor, preferred_element_type=F32).astype(BF16)
    half_left = jnp.einsum("ckl,ka->cal", slab, det_row_factor, preferred_element_type=F32).astype(BF16)
    cubes = jnp.einsum("cbk,ka->bca", half_right, det_row_factor, preferred_element_type=F32).astype(BF16)
    right_cols = jnp.einsum("cbk,cj->bjk", half_right, col_factor, preferred_element_type=F32).astype(BF16)
    left_cols = jnp.einsum("cal,cj->ajl", half_left, col_factor, preferred_element_type=F32).astype(BF16)
    cubes, right_cols, left_cols = (
        lax.all_to_all(x.reshape((n, own) + x.shape[1:]), "row", split_axis=0, concat_axis=0, tiled=True)
        for x in (cubes, right_cols, left_cols)
    )
    row_unfold = jnp.einsum("rbca,cj->rjba", cubes, col_factor, preferred_element_type=F32).astype(BF16)
    col_unfold = jnp.einsum("rbca,ri->ibca", cubes, row_factor, preferred_element_type=F32).astype(BF16)
    det_right = jnp.einsum("rbjk,ri->ibjk", right_cols, row_factor, preferred_element_type=F32).astype(BF16)
    det_left = jnp.einsum("rajl,ri->iajl", left_cols, row_factor, preferred_element_type=F32).astype(BF16)
    row_gram = jnp.einsum("rjba,sjba->rs", row_unfold, row_unfold, preferred_element_type=F32)
    col_gram = jnp.einsum("ibca,ibda->cd", col_unfold, col_unfold, preferred_element_type=F32)
    right_gram = jnp.einsum("ibjk,ibjm->km", det_right, det_right, preferred_element_type=F32)
    left_gram = jnp.einsum("iajl,iajm->lm", det_left, det_left, preferred_element_type=F32)
    scaled = (row_gram * SCAN_SCALE, col_gram * SCAN_SCALE, right_gram * DET_SCALE, left_gram * DET_SCALE)
    return lax.psum(scaled, "row")


def solution(mesh):
    in_specs = (
        P(("slab", "row"), None, None, None),
        P("slab", None),
        P("slab", None),
        P("slab", None),
        P("slab", None),
    )
    out_specs = (P("slab", None), P("slab", None), P("slab", None), P("slab", None))
    n = mesh.shape["row"]
    plane = round(n**0.5)
    tuned = plane * plane == n and n & (n - 1) == 0 and DET_RANK % (2 * n) == 0
    run = functools.partial(local, n, plane) if tuned else functools.partial(plain, n)
    return jax.shard_map(run, mesh=mesh, in_specs=in_specs, out_specs=out_specs, check_vma=False)
```

```python
import functools

import jax
import jax.numpy as jnp
from jax import lax
from jax.experimental import pallas as pl
from jax.experimental.pallas import tpu as pltpu
from jax.sharding import PartitionSpec as P

DET_RANK = 64
SCAN_RANK = 8
SCAN_SCALE = 1.0 / (SCAN_RANK * DET_RANK * DET_RANK)
DET_SCALE = 1.0 / (SCAN_RANK * SCAN_RANK * DET_RANK)
LANES = 128
GROUP = 16
BF16 = jnp.bfloat16
F32 = jnp.float32
LAST = (((1,), (1,)), ((), ()))
FIRST = (((0,), (0,)), ((), ()))


def dot(x, y, dims=None):
    if dims is None:
        return jnp.dot(x, y, preferred_element_type=F32)
    return lax.dot_general(x, y, dims, preferred_element_type=F32)


def paired(x):
    none = jnp.zeros_like(x)
    return jnp.concatenate([jnp.concatenate([x, none], 1), jnp.concatenate([none, x], 1)], 0)


def four_images(images, c):
    return jnp.concatenate(
        [
            jnp.concatenate([images[c], images[c + 1]], axis=1),
            jnp.concatenate([images[c + 2], images[c + 3]], axis=1),
        ],
        axis=0,
    )


def early_cubes(early, own, slab, dt_in, vt_in, *refs):
    *first, kept, dt2, vt2, dd, dt, vt, images, right, arrived, ready = refs
    pixels = slab.shape[1]
    plane, rank = first[0].shape[0], dt.shape[0]
    pitch = early + 1
    cuts = [0, early // 2, early]
    copies = [
        pltpu.make_async_copy(slab.at[pl.ds(a, b - a)], images.at[pl.ds(a, b - a)], arrived.at[i])
        for i, (a, b) in enumerate(zip(cuts, cuts[1:]))
    ]
    factors = [pltpu.make_async_copy(x, y, ready.at[i]) for i, (x, y) in enumerate([(dt_in, dt), (vt_in, vt)])]
    for copy in factors + copies:
        copy.start()
    for copy in factors:
        copy.wait()
    dt2[...], vt2[...] = (paired(slot_order(x[...], own)) for x in (dt, vt))
    dd[...] = paired(dt[...].T)
    for at, copy in enumerate(copies):
        copy.wait()
        for c in range(cuts[at], cuts[at + 1], 4):
            rights = dot(vt2[...], four_images(images, c), LAST)
            for i in range(2):
                for j in range(2):
                    right[pl.ds(c + 2 * i + j, rank, stride=pitch), :] = rights[
                        j * rank : (j + 1) * rank, i * pixels : (i + 1) * pixels
                    ]
    for slot in range(rank // own):
        to = first[slot // plane].at[slot % plane]
        for h in range(own // 2):
            b = slot * own + 2 * h
            x = [right[pl.ds((b + k) * pitch, early), :] for k in range(2)]
            x = jnp.concatenate(x, axis=1).astype(BF16)
            kept[b // 2] = x
            to[pl.ds(h * early, early), :] = dot(x, dd[...]).astype(BF16)


def slot_order(factor, own):
    shape = (factor.shape[0], factor.shape[0])
    r = lax.broadcasted_iota(jnp.int32, shape, 0)
    c = lax.broadcasted_iota(jnp.int32, shape, 1)
    take = (c // own == r // own ^ lax.axis_index("row")) & (c % own == r % own)
    return dot(take.astype(BF16), factor).astype(BF16)


def late_cubes(own, images, cft, dt2, vt2, dd, kept, out, right, left, second, sent):
    cols, pixels, rank = images.shape[0], images.shape[1], dt2.shape[0] // 2
    early = kept.shape[1]
    late = cols - early
    for c in range(0, cols, 4):
        four = four_images(images, c)
        lefts = dot(dt2[...], four)
        if c >= early:
            rights = dot(vt2[...], four, LAST)
        for i in range(2):
            for j in range(2):
                at = c + 2 * i + j
                left[pl.ds(at, rank, stride=cols + 1), :] = lefts[
                    i * rank : (i + 1) * rank, j * pixels : (j + 1) * pixels
                ]
                if c >= early:
                    right[pl.ds(at - early, rank, stride=late + 1), :] = rights[
                        j * rank : (j + 1) * rank, i * pixels : (i + 1) * pixels
                    ]
    pairs, pair = own // 2, 2 * SCAN_RANK

    def two(ref, b, count):
        parts = [ref[pl.ds((b + k) * (count + 1), count), :] for k in range(2)]
        return jnp.concatenate(parts, axis=1).astype(BF16)

    def stacked(sums):
        return jnp.concatenate([sums[:, :pixels], sums[:, pixels:]], axis=0).astype(BF16)

    me = lax.axis_index("row")
    copies = []
    for slot in range(rank // own):
        for h in range(pairs):
            b = slot * own + 2 * h
            x = two(right, b, late)
            y = two(left, b, cols)
            at = pairs * late + h * pair
            second[slot, pl.ds(h * late, late), :] = dot(x, dd[...]).astype(BF16)
            x = jnp.concatenate([kept[b // 2], x], axis=0)
            second[slot, pl.ds(at, pair), :] = stacked(dot(cft[...], x))
            second[slot, pl.ds(at + pairs * pair, pair), :] = stacked(dot(cft[...], y))
        copies.append(pltpu.make_async_copy(second.at[slot], out.at[me ^ slot], sent.at[slot]))
        copies[-1].start()
    for copy in copies:
        copy.wait()


def projections(n, plane, early, slab, cft, dt, vt):
    cols, pixels = slab.shape[0], slab.shape[1]
    rank = dt.shape[0]
    own = rank // n
    anywhere = pl.BlockSpec(memory_space=pl.ANY)
    in_vmem = pl.BlockSpec(memory_space=pltpu.VMEM)
    params = pltpu.CompilerParams(vmem_limit_bytes=56 << 20)
    *first, kept, dt2, vt2, dd = pl.pallas_call(
        functools.partial(early_cubes, early, own),
        out_shape=[pltpu.VMEM((plane, own // 2 * early, pixels), BF16)] * (n // plane)
        + [pltpu.VMEM((rank // 2, early, 2 * pixels), BF16)]
        + [pltpu.VMEM((2 * rank, 2 * pixels), BF16)] * 2
        + [pltpu.VMEM((2 * pixels, 2 * rank), BF16)],
        in_specs=[anywhere] * 3,
        out_specs=[in_vmem] * (n // plane + 4),
        scratch_shapes=[
            pltpu.VMEM(dt.shape, BF16),
            pltpu.VMEM(vt.shape, BF16),
            pltpu.VMEM((early,) + slab.shape[1:], BF16),
            pltpu.VMEM((rank * (early + 1), pixels), F32),
            pltpu.SemaphoreType.DMA((2,)),
            pltpu.SemaphoreType.DMA((2,)),
        ],
        compiler_params=params,
    )(slab, dt, vt)
    late = cols - early
    height = own // 2 * late + 2 * own * SCAN_RANK
    second = pl.pallas_call(
        functools.partial(late_cubes, own),
        out_shape=jax.ShapeDtypeStruct((n, height, pixels), BF16),
        in_specs=[in_vmem] * 6,
        out_specs=anywhere,
        scratch_shapes=[
            pltpu.VMEM((rank * (late + 1), pixels), F32),
            pltpu.VMEM((rank * (cols + 1), pixels), F32),
            pltpu.VMEM((n, height, pixels), BF16),
            pltpu.SemaphoreType.DMA((n,)),
        ],
        compiler_params=pltpu.CompilerParams(vmem_limit_bytes=32 << 20),
    )(slab, cft, dt2, vt2, dd, kept)
    return first, second


def one_hot(shape, rows_per, cols_per):
    r = lax.broadcasted_iota(jnp.int32, shape, 0)
    c = lax.broadcasted_iota(jnp.int32, shape, 1)
    return r // rows_per == c // cols_per


def spread_weights(rft, rows, order=None):
    weights = rft[...]
    if order is not None:
        r = lax.broadcasted_iota(jnp.int32, (rows, rows), 0)
        c = lax.broadcasted_iota(jnp.int32, (rows, rows), 1)
        weights = dot(weights, (r == (c ^ order)).astype(BF16)).astype(BF16)
    tall = one_hot((SCAN_RANK * GROUP, SCAN_RANK), GROUP, 1).astype(BF16)
    wide = one_hot((rows, rows * GROUP), 1, GROUP).astype(BF16)
    weights = dot(dot(tall, weights).astype(BF16), wide)
    r = lax.broadcasted_iota(jnp.int32, weights.shape, 0)
    c = lax.broadcasted_iota(jnp.int32, weights.shape, 1)
    return jnp.where(r % GROUP == c % GROUP, weights, 0.0).astype(BF16)


def wide(get, at, size, pitch, pairs):
    return jnp.concatenate([get(at + h * pitch, size) for h in range(pairs)], axis=1)


def stack_rows(arrays, at, size):
    return jnp.concatenate([x[pl.ds(at, size), :] for x in arrays], axis=0)


def store_unfold(unfold, at, u):
    for i in range(SCAN_RANK):
        unfold[i, pl.ds(at, GROUP), :] = u[i * GROUP : (i + 1) * GROUP]


def early_grams(own, plane, rft, cft, *refs):
    *first, plain, unfold, rowpart, corner = refs
    rows = rft.shape[1]
    pairs = own // 2
    early = first[0].shape[1] // pairs
    me = lax.axis_index("row")
    mixed = spread_weights(rft, rows, me)
    plain[...] = spread_weights(rft, rows)
    slots = [first[s % plane].at[s // plane] for s in range(rows)]
    for c in range(0, early, GROUP):
        x = wide(functools.partial(stack_rows, slots), c, GROUP, early, pairs)
        store_unfold(unfold, c, dot(mixed, x).astype(BF16))
    gram = jnp.zeros((early, early), F32)
    for i in range(SCAN_RANK):
        gram += dot(unfold[i], unfold[i], LAST)
    corner[...] = gram * SCAN_SCALE
    for s in range(rows):
        x = wide(lambda at, size: slots[s][pl.ds(at, size), :], 0, early, early, pairs)
        y = dot(cft[:, :early], x)
        for h in range(pairs):
            rowpart[h, pl.ds(me ^ s, SCAN_RANK, stride=rows), :] = y[:, h * LANES : (h + 1) * LANES]


def partial_grams(own, cft, plain, early_unfold, rowpart, corner, second, keep, send, unfold, rowbuf, total):
    rows, cols, pixels = second.shape[0], cft.shape[1], second.shape[2]
    pairs, half = own // 2, cols // 2
    slots = [second.at[s] for s in range(rows)]
    for c in range(0, half, GROUP):
        x = wide(functools.partial(stack_rows, slots), c, GROUP, half, pairs)
        store_unfold(unfold, c, dot(plain[...], x).astype(BF16))
    side = jnp.zeros((half, half), F32)
    gram = jnp.zeros((half, half), F32)
    for i in range(SCAN_RANK):
        side += dot(early_unfold[i], unfold[i], LAST)
        gram += dot(unfold[i], unfold[i], LAST)
    pack(total, 0, jnp.concatenate([corner[...], side * SCAN_SCALE], axis=1), gram * SCAN_SCALE)
    for s in range(rows):
        x = wide(lambda at, size: slots[s][pl.ds(at, size), :], 0, half, half, pairs)
        y = dot(cft[:, half:], x)
        for h in range(pairs):
            rowbuf[h, pl.ds(s, SCAN_RANK, stride=rows), :] = y[:, h * LANES : (h + 1) * LANES]
    gram = jnp.zeros((rows, rows), F32)
    for i in range(SCAN_RANK):
        for h in range(pairs):
            at = pl.ds(i * rows, rows)
            x = (rowbuf[h, at, :] + rowpart[h, at, :]).astype(BF16)
            gram += dot(x, x, LAST)
    spare = jnp.concatenate([gram * SCAN_SCALE, jnp.zeros((rows, half - rows), F32)], axis=1)
    total[pl.ds(4 * half - rows, rows), pl.ds(half, half)] = spare
    n_part = own * SCAN_RANK
    for k in range(2):
        gram = jnp.zeros((pixels, pixels), F32)
        for g in range(n_part // GROUP):
            at = pairs * half + k * n_part + g * GROUP
            u = dot(plain[...], stack_rows(slots, at, GROUP)).astype(BF16)
            gram += dot(u, u, FIRST)
        gram *= DET_SCALE
        pack(total, 1 + k, gram[:half], gram[half:, half:])
    size = keep.shape[0]
    core = lax.axis_index("row") % 2
    keep[...] = total[pl.ds(pl.multiple_of(core * size, 8), size), :]
    send[...] = total[pl.ds(pl.multiple_of((1 - core) * size, 8), size), :]


def pack(total, k, top, low):
    half, part = low.shape[0], low.shape[0] // 2
    total[pl.ds(k * half, part), :] = top[:part]
    total[pl.ds(k * half + part, part), :] = jnp.concatenate([low[part:, part:], top[part:, part:]], axis=1)
    total[pl.ds(3 * half + k // 2 * part, part), pl.ds(k % 2 * half, half)] = low[:part]


def unpack(mine, other, row_out, col_out, right_out, left_out, row_gram, grams, sems):
    even = lax.axis_index("row") % 2 == 0
    total = jnp.concatenate(
        [jnp.where(even, mine[...], other[...]), jnp.where(even, other[...], mine[...])], axis=0
    )
    cols, rows = col_out.shape[0], row_out.shape[0]
    half, part = cols // 2, cols // 4
    copies = []
    for k, out in enumerate([col_out, right_out, left_out]):
        top = total[k * half : k * half + part]
        next_top = total[k * half + part : (k + 1) * half]
        low = total[3 * half + k // 2 * part :][:part, k % 2 * half : (k % 2 + 1) * half]
        side = jnp.concatenate([top[:, half:], next_top[:, half:]], axis=0).T
        last = [side[part:], low[:, part:].T, next_top[:, :part]]
        grams[k, pl.ds(0, part), :] = top
        grams[k, pl.ds(part, part), :] = jnp.concatenate([top[:, part:half].T, next_top[:, part:]], axis=1)
        grams[k, pl.ds(half, part), :] = jnp.concatenate([side[:part], low], axis=1)
        grams[k, pl.ds(half + part, part), :] = jnp.concatenate(last, axis=1)
        copies.append(pltpu.make_async_copy(grams.at[k], out, sems.at[k]))
        copies[-1].start()
    row_gram[...] = total[4 * half - rows : 4 * half, half : half + rows]
    copies.append(pltpu.make_async_copy(row_gram, row_out, sems.at[3]))
    copies[-1].start()
    for copy in copies:
        copy.wait()


def call(kernel, args, outs, scratch=(), cost=10**8):
    return pl.pallas_call(
        kernel,
        out_shape=[jax.ShapeDtypeStruct(*out) for out in outs],
        scratch_shapes=scratch,
        compiler_params=pltpu.CompilerParams(vmem_limit_bytes=40 << 20),
        cost_estimate=pl.CostEstimate(flops=cost, bytes_accessed=1 << 20, transcendentals=0),
    )(*args)


def swap(x, n, step):
    return lax.ppermute(x, "row", [(i, i ^ step) for i in range(n)])


def by_place(plane, *refs):
    before, after = refs[:-plane], refs[-plane:]
    for z, x in enumerate(before):
        for q, y in enumerate(after):
            y[z] = x[q]


def join_planes(near, *refs):
    plane = (len(refs) - near) // 2
    before, far, after = refs[:near], refs[near : near + plane], refs[near + plane :]
    for q, y in enumerate(after):
        for z, x in enumerate(before):
            y[z] = x[q]
        y[pl.ds(near, y.shape[0] - near)] = far[q][...]


def regrouped(near, far):
    plane, height, width = near[0].shape
    some = [((len(far), height, width), BF16)] * plane
    every = [((len(near) + len(far), height, width), BF16)] * plane
    far = call(functools.partial(by_place, plane), far, some, cost=4 * 10**10)
    return call(functools.partial(join_planes, len(near)), (*near, *far), every)


def all_sum(mine, other, n):
    mine = mine + swap(other, n, 1)
    step = 2
    while step < n:
        mine = mine + swap(mine, n, step)
        step *= 2
    return mine, swap(mine, n, 1)


def local(n, plane, slab, row_factor, col_factor, det_row_factor, det_col_factor):
    slab = slab.reshape(slab.shape[-3:])
    cols, pixels = slab.shape[0], slab.shape[1]
    rows = row_factor.shape[0]
    own = DET_RANK // n
    rft, cft = row_factor.T, col_factor.T
    early = cols // 2
    first, second = projections(n, plane, early, slab, cft, det_row_factor.T, det_col_factor.T)
    first = [x if z == 0 else swap(x, n, z * plane) for z, x in enumerate(first)]
    second = lax.all_to_all(second, "row", split_axis=0, concat_axis=0, tiled=True)
    first = regrouped(first[: plane // 2], first[plane // 2 :])
    first = [x if q == 0 else swap(x, n, q) for q, x in enumerate(first)]
    pairs, width = own // 2, own * DET_RANK
    row_shape = (pairs, SCAN_RANK * rows, LANES)
    shapes = [
        ((SCAN_RANK * GROUP, rows * GROUP), BF16),
        ((SCAN_RANK, early, width), BF16),
        (row_shape, F32),
        ((early, early), F32),
    ]
    known = call(functools.partial(early_grams, own, plane), (rft, cft, *first), shapes)
    scratch = [
        pltpu.VMEM((SCAN_RANK, early, width), BF16),
        pltpu.VMEM(row_shape, F32),
        pltpu.VMEM((2 * cols, pixels), F32),
    ]
    mine, other = call(
        functools.partial(partial_grams, own), (cft, *known, second), [((cols, pixels), F32)] * 2, scratch
    )
    mine, other = all_sum(mine, other, n)
    outs = [(rows, rows), (cols, cols), (pixels, pixels), (pixels, pixels)]
    in_vmem = pl.BlockSpec(memory_space=pltpu.VMEM)
    return pl.pallas_call(
        unpack,
        out_shape=[jax.ShapeDtypeStruct(shape, F32) for shape in outs],
        in_specs=[in_vmem] * 2,
        out_specs=[pl.BlockSpec(memory_space=pl.ANY)] * 4,
        scratch_shapes=[
            pltpu.VMEM((rows, rows), F32),
            pltpu.VMEM((3, cols, cols), F32),
            pltpu.SemaphoreType.DMA((4,)),
        ],
        compiler_params=pltpu.CompilerParams(vmem_limit_bytes=16 << 20),
    )(mine, other)


def plain(n, slab, row_factor, col_factor, det_row_factor, det_col_factor):
    slab = slab.reshape(slab.shape[-3:])
    rows, own = row_factor.shape[0], DET_RANK // n
    half_right = jnp.einsum("ckl,lb->cbk", slab, det_col_factor, preferred_element_type=F32).astype(BF16)
    half_left = jnp.einsum("ckl,ka->cal", slab, det_row_factor, preferred_element_type=F32).astype(BF16)
    cubes = jnp.einsum("cbk,ka->bca", half_right, det_row_factor, preferred_element_type=F32).astype(BF16)
    right_cols = jnp.einsum("cbk,cj->bjk", half_right, col_factor, preferred_element_type=F32).astype(BF16)
    left_cols = jnp.einsum("cal,cj->ajl", half_left, col_factor, preferred_element_type=F32).astype(BF16)
    cubes, right_cols, left_cols = (
        lax.all_to_all(x.reshape((n, own) + x.shape[1:]), "row", split_axis=0, concat_axis=0, tiled=True)
        for x in (cubes, right_cols, left_cols)
    )
    row_unfold = jnp.einsum("rbca,cj->rjba", cubes, col_factor, preferred_element_type=F32).astype(BF16)
    col_unfold = jnp.einsum("rbca,ri->ibca", cubes, row_factor, preferred_element_type=F32).astype(BF16)
    det_right = jnp.einsum("rbjk,ri->ibjk", right_cols, row_factor, preferred_element_type=F32).astype(BF16)
    det_left = jnp.einsum("rajl,ri->iajl", left_cols, row_factor, preferred_element_type=F32).astype(BF16)
    row_gram = jnp.einsum("rjba,sjba->rs", row_unfold, row_unfold, preferred_element_type=F32)
    col_gram = jnp.einsum("ibca,ibda->cd", col_unfold, col_unfold, preferred_element_type=F32)
    right_gram = jnp.einsum("ibjk,ibjm->km", det_right, det_right, preferred_element_type=F32)
    left_gram = jnp.einsum("iajl,iajm->lm", det_left, det_left, preferred_element_type=F32)
    scaled = (row_gram * SCAN_SCALE, col_gram * SCAN_SCALE, right_gram * DET_SCALE, left_gram * DET_SCALE)
    return lax.psum(scaled, "row")


def solution(mesh):
    in_specs = (
        P(("slab", "row"), None, None, None),
        P("slab", None),
        P("slab", None),
        P("slab", None),
        P("slab", None),
    )
    out_specs = (P("slab", None), P("slab", None), P("slab", None), P("slab", None))
    n = mesh.shape["row"]
    plane = round(n**0.5)
    tuned = plane * plane == n and n & (n - 1) == 0 and DET_RANK % (2 * n) == 0
    run = functools.partial(local, n, plane) if tuned else functools.partial(plain, n)
    return jax.shard_map(run, mesh=mesh, in_specs=in_specs, out_specs=out_specs, check_vma=False)
```

```python
import functools

import jax
import jax.numpy as jnp
from jax import lax
from jax.experimental import pallas as pl
from jax.experimental.pallas import tpu as pltpu
from jax.sharding import PartitionSpec as P

DET_RANK = 64
SCAN_RANK = 8
SCAN_SCALE = 1.0 / (SCAN_RANK * DET_RANK * DET_RANK)
DET_SCALE = 1.0 / (SCAN_RANK * SCAN_RANK * DET_RANK)
LANES = 128
GROUP = 16
BF16 = jnp.bfloat16
F32 = jnp.float32
LAST = (((1,), (1,)), ((), ()))
FIRST = (((0,), (0,)), ((), ()))


def dot(x, y, dims=None):
    if dims is None:
        return jnp.dot(x, y, preferred_element_type=F32)
    return lax.dot_general(x, y, dims, preferred_element_type=F32)


def paired(x):
    none = jnp.zeros_like(x)
    return jnp.concatenate([jnp.concatenate([x, none], 1), jnp.concatenate([none, x], 1)], 0)


def four_images(images, c):
    return jnp.concatenate(
        [
            jnp.concatenate([images[c], images[c + 1]], axis=1),
            jnp.concatenate([images[c + 2], images[c + 3]], axis=1),
        ],
        axis=0,
    )


def early_cubes(early, own, slab, dt_in, vt_in, *refs):
    *first, kept, dt2, vt2, dd, dt, vt, images, right, arrived, ready = refs
    pixels = slab.shape[1]
    plane, rank = first[0].shape[0], dt.shape[0]
    pitch = early + 1
    cuts = [0, early // 2, early]
    copies = [
        pltpu.make_async_copy(slab.at[pl.ds(a, b - a)], images.at[pl.ds(a, b - a)], arrived.at[i])
        for i, (a, b) in enumerate(zip(cuts, cuts[1:]))
    ]
    factors = [pltpu.make_async_copy(x, y, ready.at[i]) for i, (x, y) in enumerate([(dt_in, dt), (vt_in, vt)])]
    for copy in factors + copies:
        copy.start()
    for copy in factors:
        copy.wait()
    dt2[...], vt2[...] = (paired(slot_order(x[...], own)) for x in (dt, vt))
    dd[...] = paired(dt[...].T)
    for at, copy in enumerate(copies):
        copy.wait()
        for c in range(cuts[at], cuts[at + 1], 4):
            rights = dot(vt2[...], four_images(images, c), LAST)
            for i in range(2):
                for j in range(2):
                    right[pl.ds(c + 2 * i + j, rank, stride=pitch), :] = rights[
                        j * rank : (j + 1) * rank, i * pixels : (i + 1) * pixels
                    ]
    for slot in range(rank // own):
        to = first[slot // plane].at[slot % plane]
        for h in range(own // 2):
            b = slot * own + 2 * h
            x = [right[pl.ds((b + k) * pitch, early), :] for k in range(2)]
            x = jnp.concatenate(x, axis=1).astype(BF16)
            kept[b // 2] = x
            to[pl.ds(h * early, early), :] = dot(x, dd[...]).astype(BF16)


def slot_order(factor, own):
    shape = (factor.shape[0], factor.shape[0])
    r = lax.broadcasted_iota(jnp.int32, shape, 0)
    c = lax.broadcasted_iota(jnp.int32, shape, 1)
    take = (c // own == r // own ^ lax.axis_index("row")) & (c % own == r % own)
    return dot(take.astype(BF16), factor).astype(BF16)


def late_cubes(own, images, cft, dt2, vt2, dd, kept, out, right, left, second, sent):
    cols, pixels, rank = images.shape[0], images.shape[1], dt2.shape[0] // 2
    early = kept.shape[1]
    late = cols - early
    for c in range(0, cols, 4):
        four = four_images(images, c)
        lefts = dot(dt2[...], four)
        if c >= early:
            rights = dot(vt2[...], four, LAST)
        for i in range(2):
            for j in range(2):
                at = c + 2 * i + j
                left[pl.ds(at, rank, stride=cols + 1), :] = lefts[
                    i * rank : (i + 1) * rank, j * pixels : (j + 1) * pixels
                ]
                if c >= early:
                    right[pl.ds(at - early, rank, stride=late + 1), :] = rights[
                        j * rank : (j + 1) * rank, i * pixels : (i + 1) * pixels
                    ]
    pairs, pair = own // 2, 2 * SCAN_RANK

    def two(ref, b, count):
        parts = [ref[pl.ds((b + k) * (count + 1), count), :] for k in range(2)]
        return jnp.concatenate(parts, axis=1).astype(BF16)

    def stacked(sums):
        return jnp.concatenate([sums[:, :pixels], sums[:, pixels:]], axis=0).astype(BF16)

    me = lax.axis_index("row")
    copies = []
    for slot in range(rank // own):
        for h in range(pairs):
            b = slot * own + 2 * h
            x = two(right, b, late)
            y = two(left, b, cols)
            at = pairs * late + h * pair
            second[slot, pl.ds(h * late, late), :] = dot(x, dd[...]).astype(BF16)
            sums = dot(cft[:, :early], kept[b // 2]) + dot(cft[:, early:], x)
            second[slot, pl.ds(at, pair), :] = stacked(sums)
            second[slot, pl.ds(at + pairs * pair, pair), :] = stacked(dot(cft[...], y))
        copies.append(pltpu.make_async_copy(second.at[slot], out.at[me ^ slot], sent.at[slot]))
        copies[-1].start()
    for copy in copies:
        copy.wait()


def projections(n, plane, early, slab, cft, dt, vt):
    cols, pixels = slab.shape[0], slab.shape[1]
    rank = dt.shape[0]
    own = rank // n
    anywhere = pl.BlockSpec(memory_space=pl.ANY)
    in_vmem = pl.BlockSpec(memory_space=pltpu.VMEM)
    params = pltpu.CompilerParams(vmem_limit_bytes=56 << 20)
    *first, kept, dt2, vt2, dd = pl.pallas_call(
        functools.partial(early_cubes, early, own),
        out_shape=[pltpu.VMEM((plane, own // 2 * early, pixels), BF16)] * (n // plane)
        + [pltpu.VMEM((rank // 2, early, 2 * pixels), BF16)]
        + [pltpu.VMEM((2 * rank, 2 * pixels), BF16)] * 2
        + [pltpu.VMEM((2 * pixels, 2 * rank), BF16)],
        in_specs=[anywhere] * 3,
        out_specs=[in_vmem] * (n // plane + 4),
        scratch_shapes=[
            pltpu.VMEM(dt.shape, BF16),
            pltpu.VMEM(vt.shape, BF16),
            pltpu.VMEM((early,) + slab.shape[1:], BF16),
            pltpu.VMEM((rank * (early + 1), pixels), F32),
            pltpu.SemaphoreType.DMA((2,)),
            pltpu.SemaphoreType.DMA((2,)),
        ],
        compiler_params=params,
    )(slab, dt, vt)
    late = cols - early
    height = own // 2 * late + 2 * own * SCAN_RANK
    second = pl.pallas_call(
        functools.partial(late_cubes, own),
        out_shape=jax.ShapeDtypeStruct((n, height, pixels), BF16),
        in_specs=[in_vmem] * 6,
        out_specs=anywhere,
        scratch_shapes=[
            pltpu.VMEM((rank * (late + 1), pixels), F32),
            pltpu.VMEM((rank * (cols + 1), pixels), F32),
            pltpu.VMEM((n, height, pixels), BF16),
            pltpu.SemaphoreType.DMA((n,)),
        ],
        compiler_params=pltpu.CompilerParams(vmem_limit_bytes=32 << 20),
    )(slab, cft, dt2, vt2, dd, kept)
    return first, second


def one_hot(shape, rows_per, cols_per):
    r = lax.broadcasted_iota(jnp.int32, shape, 0)
    c = lax.broadcasted_iota(jnp.int32, shape, 1)
    return r // rows_per == c // cols_per


def spread_weights(rft, rows, order=None):
    weights = rft[...]
    if order is not None:
        r = lax.broadcasted_iota(jnp.int32, (rows, rows), 0)
        c = lax.broadcasted_iota(jnp.int32, (rows, rows), 1)
        weights = dot(weights, (r == (c ^ order)).astype(BF16)).astype(BF16)
    tall = one_hot((SCAN_RANK * GROUP, SCAN_RANK), GROUP, 1).astype(BF16)
    wide = one_hot((rows, rows * GROUP), 1, GROUP).astype(BF16)
    weights = dot(dot(tall, weights).astype(BF16), wide)
    r = lax.broadcasted_iota(jnp.int32, weights.shape, 0)
    c = lax.broadcasted_iota(jnp.int32, weights.shape, 1)
    return jnp.where(r % GROUP == c % GROUP, weights, 0.0).astype(BF16)


def wide(get, at, size, pitch, pairs):
    return jnp.concatenate([get(at + h * pitch, size) for h in range(pairs)], axis=1)


def stack_rows(arrays, at, size):
    return jnp.concatenate([x[pl.ds(at, size), :] for x in arrays], axis=0)


def store_unfold(unfold, at, u):
    for i in range(SCAN_RANK):
        unfold[i, pl.ds(at, GROUP), :] = u[i * GROUP : (i + 1) * GROUP]


def early_grams(own, plane, rft, cft, *refs):
    *first, plain, unfold, rowpart, corner = refs
    rows = rft.shape[1]
    pairs = own // 2
    early = first[0].shape[1] // pairs
    me = lax.axis_index("row")
    mixed = spread_weights(rft, rows, me)
    plain[...] = spread_weights(rft, rows)
    slots = [first[s % plane].at[s // plane] for s in range(rows)]
    for c in range(0, early, GROUP):
        x = wide(functools.partial(stack_rows, slots), c, GROUP, early, pairs)
        store_unfold(unfold, c, dot(mixed, x).astype(BF16))
    gram = jnp.zeros((early, early), F32)
    for i in range(SCAN_RANK):
        gram += dot(unfold[i], unfold[i], LAST)
    corner[...] = gram * SCAN_SCALE
    for s in range(rows):
        x = wide(lambda at, size: slots[s][pl.ds(at, size), :], 0, early, early, pairs)
        y = dot(cft[:, :early], x)
        for h in range(pairs):
            rowpart[h, pl.ds(me ^ s, SCAN_RANK, stride=rows), :] = y[:, h * LANES : (h + 1) * LANES]


def partial_grams(own, cft, plain, early_unfold, rowpart, corner, second, keep, send, unfold, rowbuf, total):
    rows, cols, pixels = second.shape[0], cft.shape[1], second.shape[2]
    pairs, half = own // 2, cols // 2
    slots = [second.at[s] for s in range(rows)]
    for c in range(0, half, GROUP):
        x = wide(functools.partial(stack_rows, slots), c, GROUP, half, pairs)
        store_unfold(unfold, c, dot(plain[...], x).astype(BF16))
    side = jnp.zeros((half, half), F32)
    gram = jnp.zeros((half, half), F32)
    for i in range(SCAN_RANK):
        side += dot(early_unfold[i], unfold[i], LAST)
        gram += dot(unfold[i], unfold[i], LAST)
    pack(total, 0, jnp.concatenate([corner[...], side * SCAN_SCALE], axis=1), gram * SCAN_SCALE)
    for s in range(rows):
        x = wide(lambda at, size: slots[s][pl.ds(at, size), :], 0, half, half, pairs)
        y = dot(cft[:, half:], x)
        for h in range(pairs):
            rowbuf[h, pl.ds(s, SCAN_RANK, stride=rows), :] = y[:, h * LANES : (h + 1) * LANES]
    gram = jnp.zeros((rows, rows), F32)
    for i in range(SCAN_RANK):
        for h in range(pairs):
            at = pl.ds(i * rows, rows)
            x = (rowbuf[h, at, :] + rowpart[h, at, :]).astype(BF16)
            gram += dot(x, x, LAST)
    spare = jnp.concatenate([gram * SCAN_SCALE, jnp.zeros((rows, half - rows), F32)], axis=1)
    total[pl.ds(4 * half - rows, rows), pl.ds(half, half)] = spare
    n_part = own * SCAN_RANK
    for k in range(2):
        gram = jnp.zeros((pixels, pixels), F32)
        for g in range(n_part // GROUP):
            at = pairs * half + k * n_part + g * GROUP
            u = dot(plain[...], stack_rows(slots, at, GROUP)).astype(BF16)
            gram += dot(u, u, FIRST)
        gram *= DET_SCALE
        pack(total, 1 + k, gram[:half], gram[half:, half:])
    size = keep.shape[0]
    core = lax.axis_index("row") % 2
    keep[...] = total[pl.ds(pl.multiple_of(core * size, 8), size), :]
    send[...] = total[pl.ds(pl.multiple_of((1 - core) * size, 8), size), :]


def pack(total, k, top, low):
    half, part = low.shape[0], low.shape[0] // 2
    total[pl.ds(k * half, part), :] = top[:part]
    total[pl.ds(k * half + part, part), :] = jnp.concatenate([low[part:, part:], top[part:, part:]], axis=1)
    total[pl.ds(3 * half + k // 2 * part, part), pl.ds(k % 2 * half, half)] = low[:part]


def unpack(mine, other, row_out, col_out, right_out, left_out, row_gram, grams, sems):
    even = lax.axis_index("row") % 2 == 0
    total = jnp.concatenate(
        [jnp.where(even, mine[...], other[...]), jnp.where(even, other[...], mine[...])], axis=0
    )
    cols, rows = col_out.shape[0], row_out.shape[0]
    half, part = cols // 2, cols // 4
    copies = []
    for k, out in enumerate([col_out, right_out, left_out]):
        top = total[k * half : k * half + part]
        next_top = total[k * half + part : (k + 1) * half]
        low = total[3 * half + k // 2 * part :][:part, k % 2 * half : (k % 2 + 1) * half]
        side = jnp.concatenate([top[:, half:], next_top[:, half:]], axis=0).T
        last = [side[part:], low[:, part:].T, next_top[:, :part]]
        grams[k, pl.ds(0, part), :] = top
        grams[k, pl.ds(part, part), :] = jnp.concatenate([top[:, part:half].T, next_top[:, part:]], axis=1)
        grams[k, pl.ds(half, part), :] = jnp.concatenate([side[:part], low], axis=1)
        grams[k, pl.ds(half + part, part), :] = jnp.concatenate(last, axis=1)
        copies.append(pltpu.make_async_copy(grams.at[k], out, sems.at[k]))
        copies[-1].start()
    row_gram[...] = total[4 * half - rows : 4 * half, half : half + rows]
    copies.append(pltpu.make_async_copy(row_gram, row_out, sems.at[3]))
    copies[-1].start()
    for copy in copies:
        copy.wait()


def call(kernel, args, outs, scratch=(), cost=10**8):
    return pl.pallas_call(
        kernel,
        out_shape=[jax.ShapeDtypeStruct(*out) for out in outs],
        scratch_shapes=scratch,
        compiler_params=pltpu.CompilerParams(vmem_limit_bytes=40 << 20),
        cost_estimate=pl.CostEstimate(flops=cost, bytes_accessed=1 << 20, transcendentals=0),
    )(*args)


def swap(x, n, step):
    return lax.ppermute(x, "row", [(i, i ^ step) for i in range(n)])


def by_place(plane, *refs):
    before, after = refs[:-plane], refs[-plane:]
    for z, x in enumerate(before):
        for q, y in enumerate(after):
            y[z] = x[q]


def join_planes(near, *refs):
    plane = (len(refs) - near) // 2
    before, far, after = refs[:near], refs[near : near + plane], refs[near + plane :]
    for q, y in enumerate(after):
        for z, x in enumerate(before):
            y[z] = x[q]
        y[pl.ds(near, y.shape[0] - near)] = far[q][...]


def regrouped(near, far):
    plane, height, width = near[0].shape
    some = [((len(far), height, width), BF16)] * plane
    every = [((len(near) + len(far), height, width), BF16)] * plane
    far = call(functools.partial(by_place, plane), far, some, cost=4 * 10**10)
    return call(functools.partial(join_planes, len(near)), (*near, *far), every)


def all_sum(mine, other, n):
    mine = mine + swap(other, n, 1)
    step = 2
    while step < n:
        mine = mine + swap(mine, n, step)
        step *= 2
    return mine, swap(mine, n, 1)


def local(n, plane, slab, row_factor, col_factor, det_row_factor, det_col_factor):
    slab = slab.reshape(slab.shape[-3:])
    cols, pixels = slab.shape[0], slab.shape[1]
    rows = row_factor.shape[0]
    own = DET_RANK // n
    rft, cft = row_factor.T, col_factor.T
    early = cols // 2
    first, second = projections(n, plane, early, slab, cft, det_row_factor.T, det_col_factor.T)
    first = [x if z == 0 else swap(x, n, z * plane) for z, x in enumerate(first)]
    second = lax.all_to_all(second, "row", split_axis=0, concat_axis=0, tiled=True)
    first = regrouped(first[: plane // 2], first[plane // 2 :])
    first = [x if q == 0 else swap(x, n, q) for q, x in enumerate(first)]
    pairs, width = own // 2, own * DET_RANK
    row_shape = (pairs, SCAN_RANK * rows, LANES)
    shapes = [
        ((SCAN_RANK * GROUP, rows * GROUP), BF16),
        ((SCAN_RANK, early, width), BF16),
        (row_shape, F32),
        ((early, early), F32),
    ]
    known = call(functools.partial(early_grams, own, plane), (rft, cft, *first), shapes)
    scratch = [
        pltpu.VMEM((SCAN_RANK, early, width), BF16),
        pltpu.VMEM(row_shape, F32),
        pltpu.VMEM((2 * cols, pixels), F32),
    ]
    mine, other = call(
        functools.partial(partial_grams, own), (cft, *known, second), [((cols, pixels), F32)] * 2, scratch
    )
    mine, other = all_sum(mine, other, n)
    outs = [(rows, rows), (cols, cols), (pixels, pixels), (pixels, pixels)]
    in_vmem = pl.BlockSpec(memory_space=pltpu.VMEM)
    return pl.pallas_call(
        unpack,
        out_shape=[jax.ShapeDtypeStruct(shape, F32) for shape in outs],
        in_specs=[in_vmem] * 2,
        out_specs=[pl.BlockSpec(memory_space=pl.ANY)] * 4,
        scratch_shapes=[
            pltpu.VMEM((rows, rows), F32),
            pltpu.VMEM((3, cols, cols), F32),
            pltpu.SemaphoreType.DMA((4,)),
        ],
        compiler_params=pltpu.CompilerParams(vmem_limit_bytes=16 << 20),
    )(mine, other)


def plain(n, slab, row_factor, col_factor, det_row_factor, det_col_factor):
    slab = slab.reshape(slab.shape[-3:])
    rows, own = row_factor.shape[0], DET_RANK // n
    half_right = jnp.einsum("ckl,lb->cbk", slab, det_col_factor, preferred_element_type=F32).astype(BF16)
    half_left = jnp.einsum("ckl,ka->cal", slab, det_row_factor, preferred_element_type=F32).astype(BF16)
    cubes = jnp.einsum("cbk,ka->bca", half_right, det_row_factor, preferred_element_type=F32).astype(BF16)
    right_cols = jnp.einsum("cbk,cj->bjk", half_right, col_factor, preferred_element_type=F32).astype(BF16)
    left_cols = jnp.einsum("cal,cj->ajl", half_left, col_factor, preferred_element_type=F32).astype(BF16)
    cubes, right_cols, left_cols = (
        lax.all_to_all(x.reshape((n, own) + x.shape[1:]), "row", split_axis=0, concat_axis=0, tiled=True)
        for x in (cubes, right_cols, left_cols)
    )
    row_unfold = jnp.einsum("rbca,cj->rjba", cubes, col_factor, preferred_element_type=F32).astype(BF16)
    col_unfold = jnp.einsum("rbca,ri->ibca", cubes, row_factor, preferred_element_type=F32).astype(BF16)
    det_right = jnp.einsum("rbjk,ri->ibjk", right_cols, row_factor, preferred_element_type=F32).astype(BF16)
    det_left = jnp.einsum("rajl,ri->iajl", left_cols, row_factor, preferred_element_type=F32).astype(BF16)
    row_gram = jnp.einsum("rjba,sjba->rs", row_unfold, row_unfold, preferred_element_type=F32)
    col_gram = jnp.einsum("ibca,ibda->cd", col_unfold, col_unfold, preferred_element_type=F32)
    right_gram = jnp.einsum("ibjk,ibjm->km", det_right, det_right, preferred_element_type=F32)
    left_gram = jnp.einsum("iajl,iajm->lm", det_left, det_left, preferred_element_type=F32)
    scaled = (row_gram * SCAN_SCALE, col_gram * SCAN_SCALE, right_gram * DET_SCALE, left_gram * DET_SCALE)
    return lax.psum(scaled, "row")


def solution(mesh):
    in_specs = (
        P(("slab", "row"), None, None, None),
        P("slab", None),
        P("slab", None),
        P("slab", None),
        P("slab", None),
    )
    out_specs = (P("slab", None), P("slab", None), P("slab", None), P("slab", None))
    n = mesh.shape["row"]
    plane = round(n**0.5)
    tuned = plane * plane == n and n & (n - 1) == 0 and DET_RANK % (2 * n) == 0
    run = functools.partial(local, n, plane) if tuned else functools.partial(plain, n)
    return jax.shard_map(run, mesh=mesh, in_specs=in_specs, out_specs=out_specs, check_vma=False)
```

```python
import functools

import jax
import jax.numpy as jnp
from jax import lax
from jax.experimental import pallas as pl
from jax.experimental.pallas import tpu as pltpu
from jax.sharding import PartitionSpec as P

DET_RANK = 64
SCAN_RANK = 8
SCAN_SCALE = 1.0 / (SCAN_RANK * DET_RANK * DET_RANK)
DET_SCALE = 1.0 / (SCAN_RANK * SCAN_RANK * DET_RANK)
LANES = 128
GROUP = 16
BF16 = jnp.bfloat16
F32 = jnp.float32
LAST = (((1,), (1,)), ((), ()))
FIRST = (((0,), (0,)), ((), ()))


def dot(x, y, dims=None):
    if dims is None:
        return jnp.dot(x, y, preferred_element_type=F32)
    return lax.dot_general(x, y, dims, preferred_element_type=F32)


def paired(x):
    none = jnp.zeros_like(x)
    return jnp.concatenate([jnp.concatenate([x, none], 1), jnp.concatenate([none, x], 1)], 0)


def four_images(images, c):
    return jnp.concatenate(
        [
            jnp.concatenate([images[c], images[c + 1]], axis=1),
            jnp.concatenate([images[c + 2], images[c + 3]], axis=1),
        ],
        axis=0,
    )


def early_cubes(early, own, slab, dt_in, vt_in, *refs):
    *first, kept, dt2, vt2, dd, dt, vt, images, right, arrived, ready = refs
    pixels = slab.shape[1]
    plane, rank = first[0].shape[0], dt.shape[0]
    pitch = early + 1
    cuts = [0, early // 2, early]
    copies = [
        pltpu.make_async_copy(slab.at[pl.ds(a, b - a)], images.at[pl.ds(a, b - a)], arrived.at[i])
        for i, (a, b) in enumerate(zip(cuts, cuts[1:]))
    ]
    factors = [pltpu.make_async_copy(x, y, ready.at[i]) for i, (x, y) in enumerate([(dt_in, dt), (vt_in, vt)])]
    for copy in factors + copies:
        copy.start()
    for copy in factors:
        copy.wait()
    dt2[...], vt2[...] = (paired(slot_order(x[...], own)) for x in (dt, vt))
    dd[...] = paired(dt[...].T)
    for at, copy in enumerate(copies):
        copy.wait()
        for c in range(cuts[at], cuts[at + 1], 4):
            rights = dot(vt2[...], four_images(images, c), LAST)
            for i in range(2):
                for j in range(2):
                    right[pl.ds(c + 2 * i + j, rank, stride=pitch), :] = rights[
                        j * rank : (j + 1) * rank, i * pixels : (i + 1) * pixels
                    ]
    for slot in range(rank // own):
        to = first[slot // plane].at[slot % plane]
        for h in range(own // 2):
            b = slot * own + 2 * h
            x = [right[pl.ds((b + k) * pitch, early), :] for k in range(2)]
            x = jnp.concatenate(x, axis=1).astype(BF16)
            kept[b // 2] = x
            to[pl.ds(h * early, early), :] = dot(x, dd[...]).astype(BF16)


def slot_order(factor, own):
    shape = (factor.shape[0], factor.shape[0])
    r = lax.broadcasted_iota(jnp.int32, shape, 0)
    c = lax.broadcasted_iota(jnp.int32, shape, 1)
    take = (c // own == r // own ^ lax.axis_index("row")) & (c % own == r % own)
    return dot(take.astype(BF16), factor).astype(BF16)


def late_cubes(own, images, cft, dt2, vt2, dd, kept, out, right, left, second, sent):
    cols, pixels, rank = images.shape[0], images.shape[1], dt2.shape[0] // 2
    early = kept.shape[1]
    late = cols - early
    for c in range(0, cols, 4):
        four = four_images(images, c)
        lefts = dot(dt2[...], four)
        if c >= early:
            rights = dot(vt2[...], four, LAST)
        for i in range(2):
            for j in range(2):
                at = c + 2 * i + j
                left[pl.ds(at, rank, stride=cols + 1), :] = lefts[
                    i * rank : (i + 1) * rank, j * pixels : (j + 1) * pixels
                ]
                if c >= early:
                    right[pl.ds(at - early, rank, stride=late + 1), :] = rights[
                        j * rank : (j + 1) * rank, i * pixels : (i + 1) * pixels
                    ]
    pairs, pair = own // 2, 2 * SCAN_RANK

    def two(ref, b, count):
        parts = [ref[pl.ds((b + k) * (count + 1), count), :] for k in range(2)]
        return jnp.concatenate(parts, axis=1).astype(BF16)

    def stacked(sums):
        return jnp.concatenate([sums[:, :pixels], sums[:, pixels:]], axis=0).astype(BF16)

    me = lax.axis_index("row")
    copies = []
    for slot in range(rank // own):
        for h in range(pairs):
            b = slot * own + 2 * h
            x = two(right, b, late)
            y = two(left, b, cols)
            at = pairs * late + h * pair
            second[slot, pl.ds(h * late, late), :] = dot(x, dd[...]).astype(BF16)
            x = jnp.concatenate([kept[b // 2], x], axis=0)
            second[slot, pl.ds(at, pair), :] = stacked(dot(cft[...], x))
            second[slot, pl.ds(at + pairs * pair, pair), :] = stacked(dot(cft[...], y))
        copies.append(pltpu.make_async_copy(second.at[slot], out.at[me ^ slot], sent.at[slot]))
        copies[-1].start()
    for copy in copies:
        copy.wait()


def projections(n, plane, early, slab, cft, dt, vt):
    cols, pixels = slab.shape[0], slab.shape[1]
    rank = dt.shape[0]
    own = rank // n
    anywhere = pl.BlockSpec(memory_space=pl.ANY)
    in_vmem = pl.BlockSpec(memory_space=pltpu.VMEM)
    params = pltpu.CompilerParams(vmem_limit_bytes=56 << 20)
    *first, kept, dt2, vt2, dd = pl.pallas_call(
        functools.partial(early_cubes, early, own),
        out_shape=[pltpu.VMEM((plane, own // 2 * early, pixels), BF16)] * (n // plane)
        + [pltpu.VMEM((rank // 2, early, 2 * pixels), BF16)]
        + [pltpu.VMEM((2 * rank, 2 * pixels), BF16)] * 2
        + [pltpu.VMEM((2 * pixels, 2 * rank), BF16)],
        in_specs=[anywhere] * 3,
        out_specs=[in_vmem] * (n // plane + 4),
        scratch_shapes=[
            pltpu.VMEM(dt.shape, BF16),
            pltpu.VMEM(vt.shape, BF16),
            pltpu.VMEM((early,) + slab.shape[1:], BF16),
            pltpu.VMEM((rank * (early + 1), pixels), F32),
            pltpu.SemaphoreType.DMA((2,)),
            pltpu.SemaphoreType.DMA((2,)),
        ],
        compiler_params=params,
    )(slab, dt, vt)
    late = cols - early
    height = own // 2 * late + 2 * own * SCAN_RANK
    second = pl.pallas_call(
        functools.partial(late_cubes, own),
        out_shape=jax.ShapeDtypeStruct((n, height, pixels), BF16),
        in_specs=[in_vmem] * 6,
        out_specs=anywhere,
        scratch_shapes=[
            pltpu.VMEM((rank * (late + 1), pixels), F32),
            pltpu.VMEM((rank * (cols + 1), pixels), F32),
            pltpu.VMEM((n, height, pixels), BF16),
            pltpu.SemaphoreType.DMA((n,)),
        ],
        compiler_params=pltpu.CompilerParams(vmem_limit_bytes=32 << 20),
    )(slab, cft, dt2, vt2, dd, kept)
    return first, second


def one_hot(shape, rows_per, cols_per):
    r = lax.broadcasted_iota(jnp.int32, shape, 0)
    c = lax.broadcasted_iota(jnp.int32, shape, 1)
    return r // rows_per == c // cols_per


def spread_weights(rft, rows, order=None):
    weights = rft[...]
    if order is not None:
        r = lax.broadcasted_iota(jnp.int32, (rows, rows), 0)
        c = lax.broadcasted_iota(jnp.int32, (rows, rows), 1)
        weights = dot(weights, (r == (c ^ order)).astype(BF16)).astype(BF16)
    tall = one_hot((SCAN_RANK * GROUP, SCAN_RANK), GROUP, 1).astype(BF16)
    wide = one_hot((rows, rows * GROUP), 1, GROUP).astype(BF16)
    weights = dot(dot(tall, weights).astype(BF16), wide)
    r = lax.broadcasted_iota(jnp.int32, weights.shape, 0)
    c = lax.broadcasted_iota(jnp.int32, weights.shape, 1)
    return jnp.where(r % GROUP == c % GROUP, weights, 0.0).astype(BF16)


def wide(get, at, size, pitch, pairs):
    return jnp.concatenate([get(at + h * pitch, size) for h in range(pairs)], axis=1)


def stack_rows(arrays, at, size):
    return jnp.concatenate([x[pl.ds(at, size), :] for x in arrays], axis=0)


def store_unfold(unfold, at, u):
    for i in range(SCAN_RANK):
        unfold[i, pl.ds(at, GROUP), :] = u[i * GROUP : (i + 1) * GROUP]


def early_grams(own, plane, rft, cft, *refs):
    *first, plain, unfold, rowpart, corner = refs
    rows = rft.shape[1]
    pairs = own // 2
    early = first[0].shape[1] // pairs
    me = lax.axis_index("row")
    mixed = spread_weights(rft, rows, me)
    plain[...] = spread_weights(rft, rows)
    slots = [first[s % plane].at[s // plane] for s in range(rows)]
    for c in range(0, early, GROUP):
        x = wide(functools.partial(stack_rows, slots), c, GROUP, early, pairs)
        store_unfold(unfold, c, dot(mixed, x).astype(BF16))
    gram = jnp.zeros((early, early), F32)
    for i in range(SCAN_RANK):
        gram += dot(unfold[i], unfold[i], LAST)
    corner[...] = gram * SCAN_SCALE
    for s in range(rows):
        x = wide(lambda at, size: slots[s][pl.ds(at, size), :], 0, early, early, pairs)
        y = dot(cft[:, :early], x)
        for h in range(pairs):
            rowpart[h, pl.ds(me ^ s, SCAN_RANK, stride=rows), :] = y[:, h * LANES : (h + 1) * LANES]


def partial_grams(own, cft, plain, early_unfold, rowpart, corner, second, keep, send, unfold, rowbuf, total):
    rows, cols, pixels = second.shape[0], cft.shape[1], second.shape[2]
    pairs, half = own // 2, cols // 2
    slots = [second.at[s] for s in range(rows)]
    for c in range(0, half, GROUP):
        x = wide(functools.partial(stack_rows, slots), c, GROUP, half, pairs)
        store_unfold(unfold, c, dot(plain[...], x).astype(BF16))
    side = jnp.zeros((half, half), F32)
    gram = jnp.zeros((half, half), F32)
    for i in range(SCAN_RANK):
        side += dot(early_unfold[i], unfold[i], LAST)
        gram += dot(unfold[i], unfold[i], LAST)
    pack(total, 0, jnp.concatenate([corner[...], side * SCAN_SCALE], axis=1), gram * SCAN_SCALE)
    for s in range(rows):
        x = wide(lambda at, size: slots[s][pl.ds(at, size), :], 0, half, half, pairs)
        y = dot(cft[:, half:], x)
        for h in range(pairs):
            rowbuf[h, pl.ds(s, SCAN_RANK, stride=rows), :] = y[:, h * LANES : (h + 1) * LANES]
    gram = jnp.zeros((rows, rows), F32)
    for i in range(SCAN_RANK):
        for h in range(pairs):
            at = pl.ds(i * rows, rows)
            x = (rowbuf[h, at, :] + rowpart[h, at, :]).astype(BF16)
            gram += dot(x, x, LAST)
    spare = jnp.concatenate([gram * SCAN_SCALE, jnp.zeros((rows, half - rows), F32)], axis=1)
    total[pl.ds(4 * half - rows, rows), pl.ds(half, half)] = spare
    n_part = own * SCAN_RANK
    for k in range(2):
        gram = jnp.zeros((pixels, pixels), F32)
        for g in range(n_part // GROUP):
            at = pairs * half + k * n_part + g * GROUP
            u = dot(plain[...], stack_rows(slots, at, GROUP)).astype(BF16)
            gram += dot(u, u, FIRST)
        gram *= DET_SCALE
        pack(total, 1 + k, gram[:half], gram[half:, half:])
    size = keep.shape[0]
    core = lax.axis_index("row") % 2
    keep[...] = total[pl.ds(pl.multiple_of(core * size, 8), size), :]
    send[...] = total[pl.ds(pl.multiple_of((1 - core) * size, 8), size), :]


def pack(total, k, top, low):
    half, part = low.shape[0], low.shape[0] // 2
    total[pl.ds(k * half, part), :] = top[:part]
    total[pl.ds(k * half + part, part), :] = jnp.concatenate([low[part:, part:], top[part:, part:]], axis=1)
    total[pl.ds(3 * half + k // 2 * part, part), pl.ds(k % 2 * half, half)] = low[:part]


def unpack(mine, other, row_out, col_out, right_out, left_out, row_gram, grams, sems):
    even = lax.axis_index("row") % 2 == 0
    total = jnp.concatenate(
        [jnp.where(even, mine[...], other[...]), jnp.where(even, other[...], mine[...])], axis=0
    )
    cols, rows = col_out.shape[0], row_out.shape[0]
    half, part = cols // 2, cols // 4
    copies = []
    for k, out in reversed(list(enumerate([col_out, right_out, left_out]))):
        top = total[k * half : k * half + part]
        next_top = total[k * half + part : (k + 1) * half]
        low = total[3 * half + k // 2 * part :][:part, k % 2 * half : (k % 2 + 1) * half]
        side = jnp.concatenate([top[:, half:], next_top[:, half:]], axis=0).T
        last = [side[part:], low[:, part:].T, next_top[:, :part]]
        grams[k, pl.ds(0, part), :] = top
        grams[k, pl.ds(part, part), :] = jnp.concatenate([top[:, part:half].T, next_top[:, part:]], axis=1)
        grams[k, pl.ds(half, part), :] = jnp.concatenate([side[:part], low], axis=1)
        grams[k, pl.ds(half + part, part), :] = jnp.concatenate(last, axis=1)
        copies.append(pltpu.make_async_copy(grams.at[k], out, sems.at[k]))
        copies[-1].start()
    row_gram[...] = total[4 * half - rows : 4 * half, half : half + rows]
    copies.append(pltpu.make_async_copy(row_gram, row_out, sems.at[3]))
    copies[-1].start()
    for copy in copies:
        copy.wait()


def call(kernel, args, outs, scratch=(), cost=10**8):
    return pl.pallas_call(
        kernel,
        out_shape=[jax.ShapeDtypeStruct(*out) for out in outs],
        scratch_shapes=scratch,
        compiler_params=pltpu.CompilerParams(vmem_limit_bytes=40 << 20),
        cost_estimate=pl.CostEstimate(flops=cost, bytes_accessed=1 << 20, transcendentals=0),
    )(*args)


def swap(x, n, step):
    return lax.ppermute(x, "row", [(i, i ^ step) for i in range(n)])


def by_place(plane, *refs):
    before, after = refs[:-plane], refs[-plane:]
    for z, x in enumerate(before):
        for q, y in enumerate(after):
            y[z] = x[q]


def join_planes(near, *refs):
    plane = (len(refs) - near) // 2
    before, far, after = refs[:near], refs[near : near + plane], refs[near + plane :]
    for q, y in enumerate(after):
        for z, x in enumerate(before):
            y[z] = x[q]
        y[pl.ds(near, y.shape[0] - near)] = far[q][...]


def regrouped(near, far):
    plane, height, width = near[0].shape
    some = [((len(far), height, width), BF16)] * plane
    every = [((len(near) + len(far), height, width), BF16)] * plane
    far = call(functools.partial(by_place, plane), far, some, cost=4 * 10**10)
    return call(functools.partial(join_planes, len(near)), (*near, *far), every)


def all_sum(mine, other, n):
    mine = mine + swap(other, n, 1)
    step = 2
    while step < n:
        mine = mine + swap(mine, n, step)
        step *= 2
    return mine, swap(mine, n, 1)


def local(n, plane, slab, row_factor, col_factor, det_row_factor, det_col_factor):
    slab = slab.reshape(slab.shape[-3:])
    cols, pixels = slab.shape[0], slab.shape[1]
    rows = row_factor.shape[0]
    own = DET_RANK // n
    rft, cft = row_factor.T, col_factor.T
    early = cols // 2
    first, second = projections(n, plane, early, slab, cft, det_row_factor.T, det_col_factor.T)
    first = [x if z == 0 else swap(x, n, z * plane) for z, x in enumerate(first)]
    second = lax.all_to_all(second, "row", split_axis=0, concat_axis=0, tiled=True)
    first = regrouped(first[: plane // 2], first[plane // 2 :])
    first = [x if q == 0 else swap(x, n, q) for q, x in enumerate(first)]
    pairs, width = own // 2, own * DET_RANK
    row_shape = (pairs, SCAN_RANK * rows, LANES)
    shapes = [
        ((SCAN_RANK * GROUP, rows * GROUP), BF16),
        ((SCAN_RANK, early, width), BF16),
        (row_shape, F32),
        ((early, early), F32),
    ]
    known = call(functools.partial(early_grams, own, plane), (rft, cft, *first), shapes)
    scratch = [
        pltpu.VMEM((SCAN_RANK, early, width), BF16),
        pltpu.VMEM(row_shape, F32),
        pltpu.VMEM((2 * cols, pixels), F32),
    ]
    mine, other = call(
        functools.partial(partial_grams, own), (cft, *known, second), [((cols, pixels), F32)] * 2, scratch
    )
    mine, other = all_sum(mine, other, n)
    outs = [(rows, rows), (cols, cols), (pixels, pixels), (pixels, pixels)]
    in_vmem = pl.BlockSpec(memory_space=pltpu.VMEM)
    return pl.pallas_call(
        unpack,
        out_shape=[jax.ShapeDtypeStruct(shape, F32) for shape in outs],
        in_specs=[in_vmem] * 2,
        out_specs=[pl.BlockSpec(memory_space=pl.ANY)] * 4,
        scratch_shapes=[
            pltpu.VMEM((rows, rows), F32),
            pltpu.VMEM((3, cols, cols), F32),
            pltpu.SemaphoreType.DMA((4,)),
        ],
        compiler_params=pltpu.CompilerParams(vmem_limit_bytes=16 << 20),
    )(mine, other)


def plain(n, slab, row_factor, col_factor, det_row_factor, det_col_factor):
    slab = slab.reshape(slab.shape[-3:])
    rows, own = row_factor.shape[0], DET_RANK // n
    half_right = jnp.einsum("ckl,lb->cbk", slab, det_col_factor, preferred_element_type=F32).astype(BF16)
    half_left = jnp.einsum("ckl,ka->cal", slab, det_row_factor, preferred_element_type=F32).astype(BF16)
    cubes = jnp.einsum("cbk,ka->bca", half_right, det_row_factor, preferred_element_type=F32).astype(BF16)
    right_cols = jnp.einsum("cbk,cj->bjk", half_right, col_factor, preferred_element_type=F32).astype(BF16)
    left_cols = jnp.einsum("cal,cj->ajl", half_left, col_factor, preferred_element_type=F32).astype(BF16)
    cubes, right_cols, left_cols = (
        lax.all_to_all(x.reshape((n, own) + x.shape[1:]), "row", split_axis=0, concat_axis=0, tiled=True)
        for x in (cubes, right_cols, left_cols)
    )
    row_unfold = jnp.einsum("rbca,cj->rjba", cubes, col_factor, preferred_element_type=F32).astype(BF16)
    col_unfold = jnp.einsum("rbca,ri->ibca", cubes, row_factor, preferred_element_type=F32).astype(BF16)
    det_right = jnp.einsum("rbjk,ri->ibjk", right_cols, row_factor, preferred_element_type=F32).astype(BF16)
    det_left = jnp.einsum("rajl,ri->iajl", left_cols, row_factor, preferred_element_type=F32).astype(BF16)
    row_gram = jnp.einsum("rjba,sjba->rs", row_unfold, row_unfold, preferred_element_type=F32)
    col_gram = jnp.einsum("ibca,ibda->cd", col_unfold, col_unfold, preferred_element_type=F32)
    right_gram = jnp.einsum("ibjk,ibjm->km", det_right, det_right, preferred_element_type=F32)
    left_gram = jnp.einsum("iajl,iajm->lm", det_left, det_left, preferred_element_type=F32)
    scaled = (row_gram * SCAN_SCALE, col_gram * SCAN_SCALE, right_gram * DET_SCALE, left_gram * DET_SCALE)
    return lax.psum(scaled, "row")


def solution(mesh):
    in_specs = (
        P(("slab", "row"), None, None, None),
        P("slab", None),
        P("slab", None),
        P("slab", None),
        P("slab", None),
    )
    out_specs = (P("slab", None), P("slab", None), P("slab", None), P("slab", None))
    n = mesh.shape["row"]
    plane = round(n**0.5)
    tuned = plane * plane == n and n & (n - 1) == 0 and DET_RANK % (2 * n) == 0
    run = functools.partial(local, n, plane) if tuned else functools.partial(plain, n)
    return jax.shard_map(run, mesh=mesh, in_specs=in_specs, out_specs=out_specs, check_vma=False)
```
